256 devices in a mesh: fsdp: 16 (over z_lo, y), grp: 4 (over x), tp: 4 (over z_hi, core).
Axes of the slice: x: 4, y: 4, z: 8 (z_hi: 2, z_lo: 4; z = z_hi * 4 + z_lo), core: 2. Of those that a mesh axis runs over, the one named last changes fastest.
Arguments:
- learner_input: bfloat16 [16384, 5120], P('fsdp', 'grp'), may hold values from -6 to 6
- cotangent: bfloat16 [16384, 5120], P('fsdp', 'tp'), may hold values from -6 to 6
- token_ids: int32 [16384], P('fsdp'), may hold values from 0 to 261119, as said below
- rewards: float32 [64], replicated, may hold values from -6 to 6
- group_ids: int32 [64], replicated, may hold values from 0 to 15, never falling along the last dimension, each value on 1 to 8 neighbouring positions
- weight_master: float32 [5120, 5120], P(('tp', 'fsdp'), 'grp'), may hold values from -0.078125 to 0.078125
- adam_first: float32 [5120, 5120], P(('tp', 'fsdp'), 'grp'), may hold values from -6 to 6
- adam_second: float32 [5120, 5120], P(('tp', 'fsdp'), 'grp'), may hold values from 0.01 to 1
- hidden_rows: bfloat16 [128, 5120], P(('fsdp', 'grp')), may hold values from -6 to 6
- cache_keys: bfloat16 [128, 128, 5120], P(('fsdp', 'grp'), None, 'tp'), may hold values from -360 to 360
- cache_values: bfloat16 [128, 128, 5120], P(('fsdp', 'grp'), None, 'tp'), may hold values from -6 to 6
- cache_lengths: int32 [128], P(('fsdp', 'grp')), may hold values from 1 to 128, as said below
- ssm_state: float32 [128, 128, 5120], P(('fsdp', 'grp'), None, 'tp'), may hold values from -6 to 6
- state_weight: bfloat16 [5120, 256], replicated, may hold values from -0.0078125 to 0.0078125
- decay_rate: float32 [5120], P('tp'), may hold values from 0.05 to 4
Outputs:
- new_weight: float32 [5120, 5120], P(('tp', 'fsdp'), 'grp')
- new_first: float32 [5120, 5120], P(('tp', 'fsdp'), 'grp')
- new_second: float32 [5120, 5120], P(('tp', 'fsdp'), 'grp')
- decoded: bfloat16 [128, 5120], P(('fsdp', 'grp'))
The draws below stay inside these ranges and needn't reach their ends.
Inputs may be any that keep to these rules, and one draw needn't show every extreme that they name: `token_ids`: each sequence of 256 ids holds nonzero ids on a prefix of 128 or more positions and 0 after it. `cache_lengths`: among the 2 rows of each replica one has exactly 128 live positions.
All inputs are finite; a program needn't handle non-finite values.
Results may differ from the reference program's by a relative error of at most 0.033.
Values may be sent and summed in bfloat16 or wider, within the bound.
A program may use at most 128 MiB of HBM per device.

```python
import math
import jax
import jax.numpy as jnp
import numpy as np
from jax import lax

D = 5120
HEAD = 128
NST = 128
VOCAB = 261120
SEQ = 256
STEPS = 4
R_REP = 2
LCACHE = 128
TOKENS = 16384
LEARN_ROWS = 64
GROUPS = 16
ROLL_ROWS = 128


def draw_token_ids(key, part):
    key = jax.random.fold_in(key, 5)
    length_key, token_key = jax.random.split(key)
    seq_count = TOKENS // SEQ
    lengths = jax.random.randint(length_key, (seq_count, 1), SEQ // 2, SEQ + 1)
    lengths = jnp.where(jnp.arange(seq_count)[:, None] == 0, SEQ // 2, lengths)
    token_draw = jax.random.randint(token_key, (seq_count, SEQ), 1, VOCAB)
    first_cell = (jnp.arange(seq_count)[:, None] == 0) & (jnp.arange(SEQ)[None, :] == 0)
    token_draw = jnp.where(first_cell, VOCAB - 1, token_draw)
    alive_mask = jnp.arange(SEQ)[None, :] < lengths
    return jnp.where(alive_mask, token_draw, 0).reshape(TOKENS).astype(jnp.int32)


def draw_cache_lengths(key, part):
    key = jax.random.fold_in(key, 7)
    length_key, pick_key = jax.random.split(key)
    lengths = jax.random.randint(length_key, (ROLL_ROWS,), 1, LCACHE + 1)
    picked = jax.random.randint(pick_key, (ROLL_ROWS // R_REP,), 0, R_REP)
    row_index = jnp.arange(ROLL_ROWS)
    full_row = row_index % R_REP == jnp.repeat(picked, R_REP)
    return jnp.where(full_row, LCACHE, lengths).astype(jnp.int32)


def draw_cache_keys(key, part):
    key = jax.random.fold_in(key, 11)
    base_key = jax.random.fold_in(key, 0)
    base = jnp.clip(jax.random.normal(base_key, (ROLL_ROWS, LCACHE, D), jnp.float32), -6.0, 6.0)
    return base.astype(jnp.bfloat16)


def raised(drawn, key, source, target, parts, factor):
    def block_of(axis_at):
        return (jnp.arange(drawn.shape[axis_at]) // (drawn.shape[axis_at] // parts)).reshape((-1,) + (1,) * (drawn.ndim - 1 - axis_at))

    near = jax.random.permutation(key, parts)[block_of(target)]
    other_side = (block_of(target) + parts // 2) % parts
    return jnp.where((block_of(source) == near) | (block_of(source) == other_side), factor * drawn, drawn)


def levels(own_key, extent, pieces, least, high):
    factor_of = 1.0
    for axis_at, blocks in pieces:
        heights = jax.random.uniform(jax.random.fold_in(jax.random.fold_in(own_key, 6), axis_at), (blocks,), jnp.float32, least / len(pieces), high / len(pieces))
        factor_of = factor_of * jnp.repeat(jnp.exp(heights), extent[axis_at] // blocks).reshape((-1,) + (1,) * (len(extent) - 1 - axis_at))
    return factor_of


def split_up(count, total, bound, slope):
    weights = [(1 << 20) // math.isqrt(standing ** slope) + 1 for standing in range(2, count + 1)]
    rest, holding = total - bound - (count - 1), [1] * (count - 1)
    while rest > 0:
        free = [i for i in range(count - 1) if holding[i] < bound]
        whole, left = sum([weights[i] for i in free]), rest
        for i in free:
            extra = min(bound - holding[i], max(1, left * weights[i] // whole), rest)
            holding[i] = holding[i] + extra
            rest = rest - extra
    return np.array([bound] + holding)


def uneven_parts(own_key, amount, total, bound, skew):
    if amount == 2:
        one = jax.random.randint(own_key, (), max(1, total - bound), min(bound, total - 1) + 1)
        return jnp.stack([one, total - one])
    tallies = jnp.asarray(split_up(amount, total, bound, skew), jnp.int32)
    couples = (amount - 1) // 2
    giver, taker = tallies[1:1 + 2 * couples:2], tallies[2:2 + 2 * couples:2]
    room = jnp.minimum(giver - 1, bound - taker)
    passed = jax.random.randint(jax.random.fold_in(own_key, 1), (couples,), 0, 1 << 20) % (room + 1)
    tallies = tallies.at[1:1 + 2 * couples:2].set(giver - passed).at[2:2 + 2 * couples:2].set(taker + passed)
    return tallies[jax.random.permutation(jax.random.fold_in(own_key, 2), amount)]


def noise(key, dims, deviation, limit, pieces=(), held_as=jnp.bfloat16):
    values = jax.random.normal(key, dims, jnp.float32) * deviation
    if len(pieces) > 0:
        values = levels(key, dims, pieces, -0.22, 0.18) * values
    return jnp.clip(values, min=-limit, max=limit).astype(held_as)


def bell_draw_with(rng, extent, scale, most, cuts, heavy, dtype=jnp.bfloat16):
    values = scale * jax.random.normal(rng, extent, jnp.float32)
    if cuts:
        values = values * levels(rng, extent, cuts, -0.22, 0.18)
    return jnp.clip(raised(values, jax.random.fold_in(rng, 3), *heavy), -most, most).astype(dtype)


def setup_inputs(seed: int = 0) -> dict:
    keys = jax.random.split(jax.random.key(seed), 16)
    return {
        "learner_input": noise(keys[0], (TOKENS, D), 1.0, 6.0, ((0, 16), (1, 4))),
        "cotangent": bell_draw_with(keys[1], (TOKENS, D), 1.0, 6.0, ((0, 16), (1, 4)), (0, 1, 16, 2.0)),
        "token_ids": draw_token_ids(jax.random.fold_in(keys[15], 71), 0),
        "rewards": noise(keys[3], (LEARN_ROWS,), 1.0, 6.0, (), jnp.float32),
        "group_ids": jnp.searchsorted(jnp.cumsum(uneven_parts(keys[4], GROUPS, LEARN_ROWS, min(8, LEARN_ROWS), 0)), jnp.arange(LEARN_ROWS), side="right").astype(jnp.int32),
        "weight_master": noise(keys[5], (D, D), D ** -0.5, 0.078125, ((0, 64), (1, 4)), jnp.float32),
        "adam_first": noise(keys[6], (D, D), 0.5, 6.0, ((0, 64), (1, 4)), jnp.float32),
        "adam_second": jnp.clip(jnp.exp(math.log(1.0) - 4.6051702 * jax.random.uniform(keys[7], (D, D), jnp.float32) ** levels(keys[7], (D, D), ((0, 64), (1, 4)), -0.2, 0.2)), 0.01, 1.0),
        "hidden_rows": noise(keys[8], (ROLL_ROWS, D), 1.0, 6.0, ((0, 64),)),
        "cache_keys": draw_cache_keys(jax.random.fold_in(keys[15], 71), 0),
        "cache_values": noise(keys[10], (ROLL_ROWS, LCACHE, D), 1.0, 6.0, ((0, 64), (2, 4))),
        "cache_lengths": draw_cache_lengths(jax.random.fold_in(keys[15], 71), 0),
        "ssm_state": noise(keys[12], (ROLL_ROWS, NST, D), 1.0, 6.0, ((0, 64), (2, 4)), jnp.float32),
        "state_weight": noise(keys[13], (D, 2 * NST), (D * NST) ** -0.5, 0.0078125),
        "decay_rate": jnp.clip(jnp.exp(math.log(4.0) - 4.3820266 * jax.random.uniform(keys[14], (D,), jnp.float32) ** levels(keys[14], (D,), ((0, 4),), -0.2, 0.2)), 0.05, 4.0),
    }


beta_one = 0.9
beta_two = 0.95
learn_rate = 0.001
weight_decay = 0.1
adam_eps = 1e-08
adam_step = 10.0
norm_eps = 1e-05
mask_fill = -1e+30

def group_advantage(rewards, group_ids):
    same_group = (group_ids[:, None] == group_ids[None, :]).astype(jnp.float32)
    group_total = lax.optimization_barrier(jnp.sum(same_group * rewards[None, :], axis=1))
    group_count = lax.optimization_barrier(jnp.sum(same_group, axis=1))
    return rewards - group_total / group_count

def attend(query_bf, key_heads, value_heads, valid_mask, own_keys, step_index):
    row_total, local_width = query_bf.shape
    head_count = key_heads.shape[2]
    query_heads = query_bf.reshape(row_total, head_count, HEAD).astype(jnp.float32)
    own_heads = own_keys.reshape(row_total, STEPS, head_count, HEAD).astype(jnp.float32)
    score_scale = 1.0 / math.sqrt(HEAD)
    cache_scores = jnp.einsum('rhd,rlhd->rhl', query_heads, key_heads.astype(jnp.float32), precision=lax.Precision.HIGHEST) * score_scale
    own_scores = jnp.einsum('rhd,rshd->rhs', query_heads, own_heads, precision=lax.Precision.HIGHEST) * score_scale
    own_valid = (jnp.arange(STEPS) <= step_index)[None, None, :]
    cache_valid = valid_mask[:, None, :]
    cache_scores = jnp.where(cache_valid, cache_scores, mask_fill)
    own_scores = jnp.where(own_valid, own_scores, mask_fill)
    score_top = jnp.maximum(lax.optimization_barrier(jnp.max(cache_scores, axis=2)), lax.optimization_barrier(jnp.max(own_scores, axis=2)))[:, :, None]
    cache_exp = jnp.where(cache_valid, jnp.exp(cache_scores - score_top), 0.0)
    own_exp = jnp.where(own_valid, jnp.exp(own_scores - score_top), 0.0)
    exp_total = lax.optimization_barrier(jnp.sum(cache_exp, axis=2, keepdims=True)) + lax.optimization_barrier(jnp.sum(own_exp, axis=2, keepdims=True))
    cache_prob = (cache_exp / exp_total).astype(jnp.bfloat16).astype(jnp.float32)
    own_prob = (own_exp / exp_total).astype(jnp.bfloat16).astype(jnp.float32)
    attended = jnp.einsum('rhl,rlhd->rhd', cache_prob, value_heads.astype(jnp.float32), precision=lax.Precision.HIGHEST)
    attended = attended + jnp.einsum('rhs,rshd->rhd', own_prob, own_heads, precision=lax.Precision.HIGHEST)
    return attended.reshape(row_total, local_width)

def ssm_update(query_vals, normed, ssm_carry, state_weight, decay_rate):
    gate_vals = jnp.dot(normed, state_weight, preferred_element_type=jnp.float32)
    in_gate = gate_vals[:, :NST]
    out_gate = gate_vals[:, NST:]
    step_size = jax.nn.softplus(query_vals)
    decay_step = jnp.exp(-decay_rate[None, :] * step_size)
    ssm_carry = decay_step[:, None, :] * ssm_carry + in_gate[:, :, None] * (step_size * query_vals)[:, None, :]
    ssm_out = jnp.einsum('rk,rkc->rc', out_gate, ssm_carry, precision=lax.Precision.HIGHEST)
    return (ssm_out, ssm_carry)

def decode_rows(hidden_rows, cache_keys, cache_values, cache_lengths, ssm_state, state_weight, decay_rate, serving_weight):
    row_total, cache_size, local_width = cache_keys.shape
    head_count = local_width // HEAD
    key_heads = cache_keys.reshape(row_total, cache_size, head_count, HEAD)
    value_heads = cache_values.reshape(row_total, cache_size, head_count, HEAD)
    valid_mask = jnp.arange(cache_size)[None, :] < cache_lengths[:, None]
    own_keys = jnp.zeros((row_total, STEPS, local_width), jnp.bfloat16)
    hidden = hidden_rows.astype(jnp.float32)
    ssm_carry = ssm_state
    for step_index in range(STEPS):
        normed = (hidden * lax.rsqrt(lax.optimization_barrier(jnp.mean(hidden * hidden, axis=1, keepdims=True)) + norm_eps)).astype(jnp.bfloat16)
        query_vals = lax.dot_general(normed, serving_weight, (((1,), (1,)), ((), ())), preferred_element_type=jnp.float32)
        query_bf = query_vals.astype(jnp.bfloat16)
        own_keys = own_keys.at[:, step_index].set(query_bf)
        attended = attend(query_bf, key_heads, value_heads, valid_mask, own_keys, step_index)
        ssm_out, ssm_carry = ssm_update(query_vals, normed, ssm_carry, state_weight, decay_rate)
        mixed_out = (attended + ssm_out).astype(jnp.bfloat16)
        hidden = hidden + jnp.dot(mixed_out, serving_weight, preferred_element_type=jnp.float32)
    return hidden.astype(jnp.bfloat16)

def reference(learner_input, cotangent, token_ids, rewards, group_ids, weight_master, adam_first, adam_second, hidden_rows, cache_keys, cache_values, cache_lengths, ssm_state, state_weight, decay_rate):
    advantage = group_advantage(rewards, group_ids)
    token_adv = jnp.repeat(advantage, SEQ)
    token_weight = jnp.where(token_ids != 0, token_adv, 0.0) / SEQ
    signal = (token_weight[:, None] * cotangent.astype(jnp.float32)).astype(jnp.bfloat16)
    gradient = jnp.dot(signal.T, learner_input, preferred_element_type=jnp.float32)
    new_first = beta_one * adam_first + (1.0 - beta_one) * gradient
    new_second = beta_two * adam_second + (1.0 - beta_two) * gradient * gradient
    update = new_first / (1.0 - beta_one ** adam_step) / (jnp.sqrt(new_second / (1.0 - beta_two ** adam_step)) + adam_eps)
    new_weight = weight_master - learn_rate * (update + weight_decay * weight_master)
    serving_weight = new_weight.astype(jnp.bfloat16)
    decoded = decode_rows(hidden_rows, cache_keys, cache_values, cache_lengths, ssm_state, state_weight, decay_rate, serving_weight)
    return (new_weight, new_first, new_second, decoded)
```

```python
import functools
import math

import jax
import jax.numpy as jnp
from jax import lax
from jax.experimental import pallas as pl
from jax.experimental.pallas import tpu as pltpu
from jax.sharding import PartitionSpec as P

F32 = jnp.float32
BF16 = jnp.bfloat16
MESH = pl.DeviceIdType.MESH

D = 5120
HEAD = 128
NST = 128
SEQ = 256
STEPS = 4
BLK = 1280
SH = 80
TOK = 1024
CW = 256
CHUNKS = BLK // CW
HW = CW // 2
LC = 128
HEADS = BLK // HEAD
QW = BLK + 2 * NST + 128

beta_one = 0.9
beta_two = 0.95
learn_rate = 0.001
weight_decay = 0.1
adam_eps = 1e-08
adam_step = 10.0
norm_eps = 1e-05
mask_fill = -1e30

NT = (((1,), (1,)), ((), ()))


def kernel(
    inp_h, cot_h, ids_ref, rrow_ref, rcol_ref, grow_ref, gcol_ref,
    wm_h, m1_h, m2_h, hid_h, ck_h, cv_h, len_ref, st_h, sw_h, dec_ref,
    nw_h, nf_h, ns_h, out_ref,
    inp, cot, sigt, grad, wblk, ry, rz, zacc,
    wm, m1, m2, nw, nf, ns, hsrc, hbuf, ck, cv, st, sw,
    hid, own, qsend, qrecv, mixbuf, mix8, ps, c1r, c2s, c2r, tot, fbuf,
    lsem, ysend, yrecv, zsend, zrecv, azs, azr, ays, ayr,
    hs_s, hs_r, qs_s, qs_r, ms_s, ms_r, cs_s, cs_r, fs_s, fs_r,
):
    fs = lax.axis_index("fsdp")
    g = lax.axis_index("grp")
    tp = lax.axis_index("tp")
    z, y = fs // 4, fs % 4
    zhi, core = tp // 2, tp % 2

    def at_y(d):
        return {"fsdp": z * 4 + (y + d) % 4}

    def at_z(d):
        return {"fsdp": ((z + d) % 4) * 4 + y}

    def at_g(d):
        return {"grp": (g + d) % 4}

    mate = {"tp": zhi * 2 + (1 - core)}
    far = {"tp": (1 - zhi) * 2 + core}

    def send(src, dst, ssem, rsem, where):
        return pltpu.make_async_remote_copy(
            src_ref=src, dst_ref=dst, send_sem=ssem, recv_sem=rsem,
            device_id=where, device_id_type=MESH,
        )

    loads = [
        pltpu.make_async_copy(cot_h, cot, lsem.at[0]),
        pltpu.make_async_copy(inp_h, inp, lsem.at[1]),
        pltpu.make_async_copy(hid_h, hsrc, lsem.at[2]),
        pltpu.make_async_copy(wm_h, wm, lsem.at[3]),
        pltpu.make_async_copy(m1_h, m1, lsem.at[4]),
        pltpu.make_async_copy(m2_h, m2, lsem.at[5]),
        pltpu.make_async_copy(ck_h, ck, lsem.at[6]),
        pltpu.make_async_copy(cv_h, cv, lsem.at[7]),
        pltpu.make_async_copy(st_h, st, lsem.at[8]),
        pltpu.make_async_copy(
            sw_h.at[pl.ds(pl.multiple_of(g * BLK, BLK), BLK), :], sw, lsem.at[9]
        ),
    ]
    for copy in loads:
        copy.start()

    barrier = pltpu.get_barrier_semaphore()
    greeted = [at_y(1), at_y(3), at_z(1), at_z(3), at_g(1), at_g(2), at_g(3), mate, far]
    for where in greeted:
        pl.semaphore_signal(barrier, inc=1, device_id=where, device_id_type=MESH)

    same = (gcol_ref[...] == grow_ref[...]).astype(F32)
    adv = rrow_ref[...] - jnp.sum(same * rcol_ref[...], axis=0, keepdims=True) / jnp.sum(
        same, axis=0, keepdims=True
    )
    mine = lax.broadcasted_iota(jnp.int32, (8, 64), 1) == fs * 4 + (
        lax.broadcasted_iota(jnp.int32, (8, 64), 0) // 2
    )
    adv8 = jnp.sum(jnp.where(mine, jnp.broadcast_to(adv, (8, 64)), 0.0), axis=1, keepdims=True)
    tw = jnp.where(ids_ref[...] != 0, jnp.broadcast_to(adv8, (8, 128)), 0.0) / SEQ

    own[...] = jnp.zeros_like(own)

    loads[0].wait()

    def turn(j, _):
        col = pl.multiple_of(j * 128, 128)
        for k in range(TOK // 128):
            part = cot[k * 128 : (k + 1) * 128, pl.ds(col, 128)].T
            sigt[pl.ds(col, 128), k * 128 : (k + 1) * 128] = (
                part.astype(F32) * tw[k : k + 1, :]
            ).astype(BF16)
        return 0

    lax.fori_loop(0, BLK // 128, turn, 0)
    loads[1].wait()

    def gradient_chunk(c):
        def rows(q, _):
            part = jnp.dot(
                sigt[pl.ds(pl.multiple_of(q * 320, 320), 320), :],
                inp[:, c * CW : (c + 1) * CW],
                preferred_element_type=F32,
            )
            grad[q, :, :, c * CW : (c + 1) * CW] = part.astype(BF16).reshape(4, SH, CW)
            return 0

        lax.fori_loop(0, 4, rows, 0)

    wview = wblk.reshape(4, 4, SH, BLK)
    sent = []

    def go(copy):
        copy.start()
        sent.append(copy)
        return copy

    ylast, zlast, azlast, aylast = {}, {}, {}, {}

    def y_ring(c, s):
        for way, d in ((0, 1), (1, 3)):
            cols = pl.ds(c * CW + way * HW, HW)
            block = (y + 4 * (s + 1) - d * (s + 1)) % 4
            if s == 0:
                src = grad.at[:, block, :, cols]
            else:
                ylast[c, way].wait_recv()
                src = ry.at[c, s - 1, way]
                src[...] = (
                    src[...].astype(F32) + grad[:, block, :, c * CW + way * HW : c * CW + (way + 1) * HW].astype(F32)
                ).astype(BF16)
            ylast[c, way] = go(
                send(src, ry.at[c, s, way], ysend.at[c, s, way], yrecv.at[c, s, way], at_y(d))
            )

    def z_ring(c, s):
        block = (z + 3 - s) % 4
        if s == 0:
            for way in (0, 1):
                ylast[c, way].wait_recv()
                zacc[c, :, :, way * HW : (way + 1) * HW] = (
                    ry[c, 2, way].astype(F32)
                    + grad[:, y, :, c * CW + way * HW : c * CW + (way + 1) * HW].astype(F32)
                ).astype(BF16)
            src = zacc.at[c, block]
        else:
            zlast[c].wait_recv()
            src = rz.at[c, s - 1]
            src[...] = (src[...].astype(F32) + zacc[c, block].astype(F32)).astype(BF16)
        zlast[c] = go(send(src, rz.at[c, s], zsend.at[c, s], zrecv.at[c, s], at_z(1)))

    def adam(c):
        cols = slice(c * CW, (c + 1) * CW)
        zlast[c].wait_recv()
        grad_sum = rz[c, 2].astype(F32) + zacc[c, z].astype(F32)
        if c == 0:
            for copy in loads[3:6]:
                copy.wait()
        first = beta_one * m1[:, cols] + (1.0 - beta_one) * grad_sum
        second = beta_two * m2[:, cols] + (1.0 - beta_two) * grad_sum * grad_sum
        update = (
            first
            / (1.0 - beta_one**adam_step)
            / (jnp.sqrt(second / (1.0 - beta_two**adam_step)) + adam_eps)
        )
        master = wm[:, cols]
        fresh = master - learn_rate * (update + weight_decay * master)
        nf[:, cols] = first
        ns[:, cols] = second
        nw[:, cols] = fresh
        wblk[pl.ds(pl.multiple_of(fs * SH, 16), SH), cols] = fresh.astype(BF16)

    def z_gather(c, s):
        if s > 0:
            azlast[c].wait_recv()
        place = wview.at[(z + 4 - s) % 4, y, :, pl.ds(c * CW, CW)]
        azlast[c] = go(send(place, place, azs.at[c, s], azr.at[c, s], at_z(1)))

    def y_gather(c, s):
        if s == 0:
            azlast[c].wait_recv()
        for way, d in ((0, 1), (1, 3)):
            if s > 0:
                aylast[c, way].wait_recv()
            place = wview.at[:, (y + 4 * s - d * s) % 4, :, pl.ds(c * CW + way * HW, HW)]
            aylast[c, way] = go(
                send(place, place, ays.at[c, s, way], ayr.at[c, s, way], at_y(d))
            )

    def stage(c, s):
        if s < 3:
            y_ring(c, s)
        elif s < 6:
            z_ring(c, s - 3)
        elif s < 9:
            if s == 6:
                adam(c)
            z_gather(c, s - 6)
        elif s < 12:
            y_gather(c, s - 9)
        else:
            aylast[c, 0].wait_recv()
            aylast[c, 1].wait_recv()

    stores = [
        pltpu.make_async_copy(nw, nw_h, lsem.at[10]),
        pltpu.make_async_copy(nf, nf_h, lsem.at[11]),
        pltpu.make_async_copy(ns, ns_h, lsem.at[12]),
    ]
    for t in range(13 + CHUNKS - 1):
        if t < CHUNKS:
            gradient_chunk(t)
        if t == 0:
            loads[2].wait()
            pl.semaphore_wait(barrier, len(greeted))
        for c in range(CHUNKS):
            if 0 <= t - c < 13:
                stage(c, t - c)
        if t == 0:
            hcopies = [
                send(hsrc.at[(g + d) % 4], hbuf.at[g], hs_s.at[d - 1], hs_r.at[d - 1], at_g(d))
                for d in (1, 2, 3)
            ]
            for copy in hcopies:
                copy.start()
            hbuf[g] = hsrc[g]
        if t == 6 + CHUNKS - 1:
            for copy in stores:
                copy.start()

    for copy in hcopies:
        copy.wait()
    for i in range(4):
        hid[2 * i : 2 * i + 2, :] = hbuf[i]
    for copy in loads[6:]:
        copy.wait()

    head_of = (
        lax.broadcasted_iota(jnp.int32, (16, BLK), 1) // HEAD
        == lax.broadcasted_iota(jnp.int32, (16, BLK), 0)
    )
    own_row = lax.broadcasted_iota(jnp.int32, (16, BLK), 0)
    place128 = lax.broadcasted_iota(jnp.int32, (16, LC), 1)
    place16 = lax.broadcasted_iota(jnp.int32, (16, 16), 1)
    score_scale = 1.0 / math.sqrt(HEAD)

    def decode_step(s, _):
        h = hid[...]
        high = h.astype(BF16).astype(F32)
        both = jnp.concatenate([high, h - high], axis=0).astype(BF16)
        for n in range(CHUNKS):
            part = lax.dot_general(
                both, wblk[n * 256 : (n + 1) * 256, :], NT, preferred_element_type=F32
            )
            part = part[0:8] + part[8:16]
            for i in range(4):
                qsend[s, i, :, n * 256 : (n + 1) * 256] = part[2 * i : 2 * i + 2]
        part = jnp.dot(both, sw[...], preferred_element_type=F32)
        part = part[0:8] + part[8:16]
        square = jnp.broadcast_to(jnp.sum(h * h, axis=1, keepdims=True), (8, 128))
        for i in range(4):
            qsend[s, i, :, BLK : BLK + 2 * NST] = part[2 * i : 2 * i + 2]
            qsend[s, i, :, BLK + 2 * NST :] = square[2 * i : 2 * i + 2]
        copies = [
            send(
                qsend.at[s, (g + d) % 4], qrecv.at[s, d - 1],
                qs_s.at[s, d - 1], qs_r.at[s, d - 1], at_g(d),
            )
            for d in (1, 2, 3)
        ]
        for copy in copies:
            copy.start()
        total = qsend[s, g]
        for d, copy in enumerate(copies):
            copy.wait_recv()
            total = total + qrecv[s, d]
        scale = lax.rsqrt(total[:, BLK + 2 * NST : BLK + 2 * NST + 1] * (1.0 / D) + norm_eps)
        query = total[:, 0:BLK] * scale
        gates = total[:, BLK : BLK + 2 * NST] * scale
        query_bf = query.astype(BF16).astype(F32)
        step_size = jnp.maximum(query, 0.0) + jnp.log1p(jnp.exp(-jnp.abs(query)))
        decay = jnp.exp(-dec_ref[...] * step_size)
        drive = step_size * query

        for r in range(2):
            qrow = jnp.broadcast_to(query_bf[r : r + 1, :], (16, BLK))
            own_now = jnp.where(own_row == s, qrow, own[r])
            own[r] = own_now
            own_bf = own_now.astype(BF16)
            qhead = jnp.where(head_of, qrow, 0.0).astype(BF16)
            live = place128 < len_ref[r]
            mine_live = place16 <= s
            score = lax.dot_general(qhead, ck[r], NT, preferred_element_type=F32) * score_scale
            score_own = lax.dot_general(qhead, own_bf, NT, preferred_element_type=F32) * score_scale
            score = jnp.where(live, score, mask_fill)
            score_own = jnp.where(mine_live, score_own, mask_fill)
            top = jnp.maximum(
                jnp.max(score, axis=1, keepdims=True), jnp.max(score_own, axis=1, keepdims=True)
            )
            weight = jnp.where(live, jnp.exp(score - top), 0.0)
            weight_own = jnp.where(mine_live, jnp.exp(score_own - top), 0.0)
            norm = jnp.sum(weight, axis=1, keepdims=True) + jnp.sum(
                weight_own, axis=1, keepdims=True
            )
            prob = (weight / norm).astype(BF16)
            prob_own = (weight_own / norm).astype(BF16)
            attended = jnp.dot(prob, cv[r], preferred_element_type=F32) + jnp.dot(
                prob_own, own_bf, preferred_element_type=F32
            )
            attended = jnp.sum(jnp.where(head_of, attended, 0.0), axis=0, keepdims=True)
            in_gate = jnp.broadcast_to(gates[r : r + 1, 0:NST], (NST, NST)).T
            out_gate = jnp.broadcast_to(gates[r : r + 1, NST:], (NST, NST)).T
            for j in range(HEADS):
                cols = slice(j * 128, (j + 1) * 128)
                now = decay[r : r + 1, cols] * st[r, :, cols] + in_gate * drive[r : r + 1, cols]
                st[r, :, cols] = now
                mixed = attended[:, cols] + jnp.sum(out_gate * now, axis=0, keepdims=True)
                mixbuf[s, g, r : r + 1, cols] = mixed.astype(BF16).astype(F32)

        copies2 = [
            send(
                mixbuf.at[s, g], mixbuf.at[s, g],
                ms_s.at[s, d - 1], ms_r.at[s, d - 1], at_g(d),
            )
            for d in (1, 2, 3)
        ]
        for copy in copies2:
            copy.start()
        for copy in copies2:
            copy.wait_recv()
        for i in range(4):
            mix8[2 * i : 2 * i + 2, :] = mixbuf[s, i]
        lhs = mix8[...].astype(BF16)

        def half(which):
            cols = pl.ds(pl.multiple_of(which * 640, 128), 640)
            return jnp.dot(lhs, wblk[:, cols], preferred_element_type=F32)

        ps[s] = half(1 - core)
        one = send(ps.at[s], c1r.at[s], cs_s.at[s, 0], cs_r.at[s, 0], mate)
        one.start()
        mine_half = half(core)
        one.wait_recv()
        c2s[s] = mine_half + c1r[s]
        two = send(c2s.at[s], c2r.at[s], cs_s.at[s, 1], cs_r.at[s, 1], far)
        two.start()
        two.wait_recv()
        tot[s, core] = c2s[s] + c2r[s]
        three = send(tot.at[s, core], tot.at[s, core], cs_s.at[s, 2], cs_r.at[s, 2], mate)
        three.start()
        three.wait_recv()
        hid[:, 0:640] = hid[:, 0:640] + tot[s, 0]
        hid[:, 640:] = hid[:, 640:] + tot[s, 1]
        for copy in copies + copies2 + [one, two, three]:
            copy.wait_send()
        return 0

    lax.fori_loop(0, STEPS, decode_step, 0)

    for i in range(4):
        hsrc[i] = hid[2 * i : 2 * i + 2, :]
    last = [
        go(send(hsrc.at[(g + d) % 4], fbuf.at[g], fs_s.at[d - 1], fs_r.at[d - 1], at_g(d)))
        for d in (1, 2, 3)
    ]
    fbuf[g] = hsrc[g]
    for copy in last:
        copy.wait_recv()
    for i in range(4):
        out_ref[:, i * BLK : (i + 1) * BLK] = fbuf[i].astype(BF16)
    for copy in stores:
        copy.wait()
    for copy in sent:
        copy.wait_send()


def on_device(
    learner_input, cotangent, token_ids, rewards, group_ids, weight_master, adam_first,
    adam_second, hidden_rows, cache_keys, cache_values, cache_lengths, ssm_state,
    state_weight, decay_rate,
):
    hidden = hidden_rows.astype(F32).reshape(2, 4, BLK).transpose(1, 0, 2)
    hbm = pl.BlockSpec(memory_space=pl.ANY)
    vmem = pl.BlockSpec(memory_space=pltpu.VMEM)
    smem = pl.BlockSpec(memory_space=pltpu.SMEM)
    dma = pltpu.SemaphoreType.DMA
    V = pltpu.VMEM
    shard = jax.ShapeDtypeStruct((SH, BLK), F32)
    return pl.pallas_call(
        kernel,
        out_shape=(shard, shard, shard, jax.ShapeDtypeStruct((2, D), BF16)),
        in_specs=[hbm, hbm] + [vmem] * 5 + [hbm] * 6 + [smem] + [hbm] * 2 + [vmem],
        out_specs=(hbm, hbm, hbm, vmem),
        scratch_shapes=[
            V((TOK, BLK), BF16), V((TOK, BLK), BF16), V((BLK, TOK), BF16),
            V((4, 4, SH, BLK), BF16), V((BLK, BLK), BF16),
            V((CHUNKS, 3, 2, 4, SH, HW), BF16), V((CHUNKS, 3, SH, CW), BF16),
            V((CHUNKS, 4, SH, CW), BF16),
            V((SH, BLK), F32), V((SH, BLK), F32), V((SH, BLK), F32),
            V((SH, BLK), F32), V((SH, BLK), F32), V((SH, BLK), F32),
            V((4, 2, BLK), F32), V((4, 2, BLK), F32),
            V((2, LC, BLK), BF16), V((2, LC, BLK), BF16), V((2, NST, BLK), F32),
            V((BLK, 2 * NST), BF16),
            V((8, BLK), F32), V((2, 16, BLK), F32),
            V((STEPS, 4, 2, QW), F32), V((STEPS, 3, 2, QW), F32),
            V((STEPS, 4, 2, BLK), F32), V((8, BLK), F32),
            V((STEPS, 8, 640), F32), V((STEPS, 8, 640), F32), V((STEPS, 8, 640), F32),
            V((STEPS, 8, 640), F32), V((STEPS, 2, 8, 640), F32), V((4, 2, BLK), F32),
            dma((13,)),
            dma((CHUNKS, 3, 2)), dma((CHUNKS, 3, 2)), dma((CHUNKS, 3)), dma((CHUNKS, 3)),
            dma((CHUNKS, 3)), dma((CHUNKS, 3)), dma((CHUNKS, 3, 2)), dma((CHUNKS, 3, 2)),
            dma((3,)), dma((3,)), dma((STEPS, 3)), dma((STEPS, 3)),
            dma((STEPS, 3)), dma((STEPS, 3)), dma((STEPS, 3)), dma((STEPS, 3)),
            dma((3,)), dma((3,)),
        ],
        compiler_params=pltpu.CompilerParams(
            collective_id=0, has_side_effects=True, vmem_limit_bytes=56 * 1024 * 1024
        ),
    )(
        learner_input, cotangent, token_ids.reshape(8, 128),
        rewards.reshape(1, 64), rewards.reshape(64, 1),
        group_ids.reshape(1, 64), group_ids.reshape(64, 1),
        weight_master, adam_first, adam_second, hidden, cache_keys, cache_values,
        cache_lengths, ssm_state, state_weight, decay_rate.reshape(1, BLK),
    )


def solution(mesh):
    in_specs = (
        P("fsdp", "grp"), P("fsdp", "tp"), P("fsdp"), P(), P(),
        P(("tp", "fsdp"), "grp"), P(("tp", "fsdp"), "grp"), P(("tp", "fsdp"), "grp"),
        P(("fsdp", "grp"), None), P(("fsdp", "grp"), None, "tp"),
        P(("fsdp", "grp"), None, "tp"), P(("fsdp", "grp")),
        P(("fsdp", "grp"), None, "tp"), P(), P("tp"),
    )
    out_specs = (
        P(("tp", "fsdp"), "grp"), P(("tp", "fsdp"), "grp"), P(("tp", "fsdp"), "grp"),
        P(("fsdp", "grp"), None),
    )
    return jax.shard_map(
        on_device, mesh=mesh, in_specs=in_specs, out_specs=out_specs, check_vma=False
    )
```

```python
import functools
import math

import jax
import jax.numpy as jnp
from jax import lax
from jax.experimental import pallas as pl
from jax.experimental.pallas import tpu as pltpu
from jax.sharding import PartitionSpec as P

F32 = jnp.float32
BF16 = jnp.bfloat16
MESH = pl.DeviceIdType.MESH

D = 5120
HEAD = 128
NST = 128
SEQ = 256
STEPS = 4
BLK = 1280
SH = 80
TOK = 1024
CW = 256
CHUNKS = BLK // CW
HW = CW // 2
LC = 128
HEADS = BLK // HEAD
QW = BLK + 2 * NST + 128

beta_one = 0.9
beta_two = 0.95
learn_rate = 0.001
weight_decay = 0.1
adam_eps = 1e-08
adam_step = 10.0
norm_eps = 1e-05
mask_fill = -1e30

NT = (((1,), (1,)), ((), ()))


def adam_update(grad, master, first, second):
    first = beta_one * first + (1.0 - beta_one) * grad
    second = beta_two * second + (1.0 - beta_two) * grad * grad
    update = (
        first
        / (1.0 - beta_one**adam_step)
        / (jnp.sqrt(second / (1.0 - beta_two**adam_step)) + adam_eps)
    )
    return master - learn_rate * (update + weight_decay * master), first, second


def finish(grad, master, first, second, rows, nw, nf, ns, out):
    nw[...], nf[...], ns[...] = adam_update(grad[...], master[...], first[...], second[...])
    out[...] = rows[...]


def kernel(
    inp_h, cot_h, ids_ref, rew_ref, grp_ref,
    wm_h, m1_h, m2_h, hid_ref, ck_h, cv_h, len_ref, st_h, sw_h, dec_ref,
    gout_h, out_ref,
    inp, cot, sigt, grad, wblk, ry, rz, zacc,
    wm, m1, m2, gsum, hsrc, hbuf, ck, cv, st, sw, dec,
    hid, own, qsend, qrecv, mixbuf, mix8, cbuf, fsrc, fbuf,
    lsem, ysend, yrecv, zsend, zrecv, azs, azr, ays, ayr,
    hs_s, hs_r, qs_s, qs_r, ms_s, ms_r, cs_s, cs_r, fs_s, fs_r,
):
    fs = lax.axis_index("fsdp")
    g = lax.axis_index("grp")
    tp = lax.axis_index("tp")
    z, y = fs // 4, fs % 4

    def at_y(d):
        return {"fsdp": z * 4 + (y + d) % 4}

    def at_z(d):
        return {"fsdp": ((z + d) % 4) * 4 + y}

    def at_g(d):
        return {"grp": (g + d) % 4}

    def at_tp(d):
        return {"tp": (tp + d) % 4}

    def send(src, dst, ssem, rsem, where):
        return pltpu.make_async_remote_copy(
            src_ref=src, dst_ref=dst, send_sem=ssem, recv_sem=rsem,
            device_id=where, device_id_type=MESH,
        )

    loads = [
        pltpu.make_async_copy(cot_h, cot, lsem.at[0]),
        pltpu.make_async_copy(inp_h, inp, lsem.at[1]),
        pltpu.make_async_copy(wm_h, wm, lsem.at[2]),
        pltpu.make_async_copy(m1_h, m1, lsem.at[3]),
        pltpu.make_async_copy(m2_h, m2, lsem.at[4]),
        pltpu.make_async_copy(ck_h, ck, lsem.at[5]),
        pltpu.make_async_copy(cv_h, cv, lsem.at[6]),
        pltpu.make_async_copy(st_h, st, lsem.at[7]),
        pltpu.make_async_copy(
            sw_h.at[pl.ds(pl.multiple_of(g * BLK, BLK), BLK), :], sw, lsem.at[8]
        ),
    ]
    for copy in loads[:2]:
        copy.start()

    barrier = pltpu.get_barrier_semaphore()
    greeted = [at_y(1), at_y(3)] + [at(d) for at in (at_z, at_g, at_tp) for d in (1, 2, 3)]
    for where in greeted:
        pl.semaphore_signal(barrier, inc=1, device_id=where, device_id_type=MESH)

    diag = lax.broadcasted_iota(jnp.int32, (64, 64), 0) == lax.broadcasted_iota(
        jnp.int32, (64, 64), 1
    )
    ids_row = jnp.broadcast_to(grp_ref[...].astype(F32), (64, 64))
    rew_row = jnp.broadcast_to(rew_ref[...], (64, 64))
    ids_col = jnp.sum(jnp.where(diag, ids_row, 0.0), axis=1, keepdims=True)
    rew_col = jnp.sum(jnp.where(diag, rew_row, 0.0), axis=1, keepdims=True)
    same = (ids_row == ids_col).astype(F32)
    adv = rew_ref[...] - jnp.sum(same * rew_col, axis=0, keepdims=True) / jnp.sum(
        same, axis=0, keepdims=True
    )
    mine = lax.broadcasted_iota(jnp.int32, (8, 64), 1) == fs * 4 + (
        lax.broadcasted_iota(jnp.int32, (8, 64), 0) // 2
    )
    adv8 = jnp.sum(jnp.where(mine, jnp.broadcast_to(adv, (8, 64)), 0.0), axis=1, keepdims=True)
    tw = jnp.where(ids_ref[...] != 0, jnp.broadcast_to(adv8, (8, 128)), 0.0) / SEQ

    for i in range(4):
        hsrc[i] = hid_ref[:, i * BLK : (i + 1) * BLK].astype(F32)
    for j in range(HEADS):
        dec[0:1, j * 128 : (j + 1) * 128] = dec_ref[j : j + 1, :]
    own[...] = jnp.zeros_like(own)

    loads[0].wait()

    def turn(j, _):
        col = pl.multiple_of(j * 128, 128)
        for k in range(TOK // 128):
            part = cot[k * 128 : (k + 1) * 128, pl.ds(col, 128)].T
            sigt[pl.ds(col, 128), k * 128 : (k + 1) * 128] = (
                part.astype(F32) * tw[k : k + 1, :]
            ).astype(BF16)
        return 0

    lax.fori_loop(0, BLK // 128, turn, 0)
    loads[1].wait()
    for copy in loads[2:]:
        copy.start()

    def gradient_chunk(c):
        def rows(q, _):
            part = jnp.dot(
                sigt[pl.ds(pl.multiple_of(q * 320, 320), 320), :],
                inp[:, c * CW : (c + 1) * CW],
                preferred_element_type=F32,
            )
            grad[q, :, :, c * CW : (c + 1) * CW] = part.astype(BF16).reshape(4, SH, CW)
            return 0

        lax.fori_loop(0, 4, rows, 0)

    wview = wblk.reshape(4, 4, SH, BLK)
    sent = []

    def go(copy):
        copy.start()
        sent.append(copy)
        return copy

    F, B = 0, HW
    ylast, zlast, azlast, aylast = {}, {}, {}, {}

    def own_part(c, block, side):
        return grad[:, block, :, c * CW + side : c * CW + side + HW].astype(F32)

    def y_send(c, k, src, d):
        ylast[c, k] = go(send(src, ry.at[c, k], ysend.at[c, k], yrecv.at[c, k], at_y(d)))

    def reduce_a(c):
        for k, block, side, d in ((0, 2, F, 1), (2, 2, B, 3), (1, 1, B, 1), (3, 3, F, 3)):
            y_send(c, k, grad.at[:, (y + block) % 4, :, pl.ds(c * CW + side, HW)], d)

    def reduce_b(c):
        for k, block, side, d in ((0, 1, F, 1), (2, 3, B, 3)):
            ylast[c, k].wait_recv()
            ry[c, k] = (ry[c, k].astype(F32) + own_part(c, (y + block) % 4, side)).astype(BF16)
            y_send(c, 4 + k // 2, ry.at[c, k], d)

    def reduce_z(c):
        for k, last, side in ((3, 4, F), (1, 5, B)):
            ylast[c, k].wait_recv()
            ylast[c, last].wait_recv()
            zacc[c, :, :, side : side + HW] = (
                own_part(c, y, side) + ry[c, k].astype(F32) + ry[c, last].astype(F32)
            ).astype(BF16)
        for d in (1, 2, 3):
            zlast[c, d] = go(
                send(
                    zacc.at[c, (z + d) % 4], rz.at[c, d - 1],
                    zsend.at[c, d - 1], zrecv.at[c, d - 1], at_z(d),
                )
            )

    def adam(c):
        cols = slice(c * CW, (c + 1) * CW)
        total = zacc[c, z].astype(F32)
        for d in (1, 2, 3):
            zlast[c, d].wait_recv()
            total = total + rz[c, d - 1].astype(F32)
        if c == 0:
            for copy in loads[2:5]:
                copy.wait()
        gsum[:, cols] = total
        fresh = adam_update(total, wm[:, cols], m1[:, cols], m2[:, cols])[0]
        wblk[pl.ds(pl.multiple_of(fs * SH, 16), SH), cols] = fresh.astype(BF16)
        for d in (1, 2, 3):
            place = wview.at[z, y, :, pl.ds(c * CW, CW)]
            azlast[c, d] = go(send(place, place, azs.at[c, d - 1], azr.at[c, d - 1], at_z(d)))

    def gather_a(c):
        for d in (1, 2, 3):
            azlast[c, d].wait_recv()
        for k, d in ((0, 1), (1, 3)):
            place = wview.at[:, y, :, pl.ds(c * CW, CW)]
            aylast[c, k] = go(send(place, place, ays.at[c, k], ayr.at[c, k], at_y(d)))

    def gather_b(c):
        for k, block, side, d in ((0, 3, F, 1), (1, 1, B, 3)):
            aylast[c, k].wait_recv()
            place = wview.at[:, (y + block) % 4, :, pl.ds(c * CW + side, HW)]
            aylast[c, k + 2] = go(
                send(place, place, ays.at[c, k + 2], ayr.at[c, k + 2], at_y(d))
            )

    def gather_end(c):
        aylast[c, 2].wait_recv()
        aylast[c, 3].wait_recv()

    stages = (reduce_a, reduce_b, reduce_z, adam, gather_a, gather_b, gather_end)
    store = pltpu.make_async_copy(gsum, gout_h, lsem.at[9])
    hcopies = [
        send(hsrc.at[(g + d) % 4], hbuf.at[g], hs_s.at[d - 1], hs_r.at[d - 1], at_g(d))
        for d in (1, 2, 3)
    ]
    for t in range(len(stages) + CHUNKS - 1):
        if t < CHUNKS:
            gradient_chunk(t)
        if t == 0:
            pl.semaphore_wait(barrier, len(greeted))
        for c in range(CHUNKS):
            if 0 <= t - c < len(stages):
                stages[t - c](c)
        if t == 0:
            for copy in hcopies:
                copy.start()
            hbuf[g] = hsrc[g]
        if t == 3 + CHUNKS - 1:
            store.start()

    for copy in hcopies:
        copy.wait()
    for i in range(4):
        hid[2 * i : 2 * i + 2, :] = hbuf[i]
    for copy in loads[5:]:
        copy.wait()

    head_of = (
        lax.broadcasted_iota(jnp.int32, (16, BLK), 1) // HEAD
        == lax.broadcasted_iota(jnp.int32, (16, BLK), 0)
    )
    own_row = lax.broadcasted_iota(jnp.int32, (16, BLK), 0)
    place128 = lax.broadcasted_iota(jnp.int32, (16, LC), 1)
    place16 = lax.broadcasted_iota(jnp.int32, (16, 16), 1)
    score_scale = 1.0 / math.sqrt(HEAD)

    def decode_step(s, _):
        h = hid[...]
        high = h.astype(BF16).astype(F32)
        both = jnp.concatenate([high, h - high], axis=0).astype(BF16)
        for n in range(CHUNKS):
            part = lax.dot_general(
                both, wblk[n * 256 : (n + 1) * 256, :], NT, preferred_element_type=F32
            )
            part = part[0:8] + part[8:16]
            for i in range(4):
                qsend[s, i, :, n * 256 : (n + 1) * 256] = part[2 * i : 2 * i + 2]
        part = jnp.dot(both, sw[...], preferred_element_type=F32)
        part = part[0:8] + part[8:16]
        square = jnp.broadcast_to(jnp.sum(h * h, axis=1, keepdims=True), (8, 128))
        for i in range(4):
            qsend[s, i, :, BLK : BLK + 2 * NST] = part[2 * i : 2 * i + 2]
            qsend[s, i, :, BLK + 2 * NST :] = square[2 * i : 2 * i + 2]
        copies = [
            send(
                qsend.at[s, (g + d) % 4], qrecv.at[s, d - 1],
                qs_s.at[s, d - 1], qs_r.at[s, d - 1], at_g(d),
            )
            for d in (1, 2, 3)
        ]
        for copy in copies:
            copy.start()
        total = qsend[s, g]
        for d, copy in enumerate(copies):
            copy.wait_recv()
            total = total + qrecv[s, d]
        scale = lax.rsqrt(total[:, BLK + 2 * NST : BLK + 2 * NST + 1] * (1.0 / D) + norm_eps)
        query = total[:, 0:BLK] * scale
        gates = total[:, BLK : BLK + 2 * NST] * scale
        query_bf = query.astype(BF16).astype(F32)
        step_size = jnp.maximum(query, 0.0) + jnp.log1p(jnp.exp(-jnp.abs(query)))
        decay = jnp.exp(-dec[...] * step_size)
        drive = step_size * query

        in_gates = []
        for r in range(2):
            qrow = jnp.broadcast_to(query_bf[r : r + 1, :], (16, BLK))
            own_now = jnp.where(own_row == s, qrow, own[r])
            own[r] = own_now
            own_bf = own_now.astype(BF16)
            qhead = jnp.where(head_of, qrow, 0.0).astype(BF16)
            live = place128 < len_ref[r]
            mine_live = place16 <= s
            score = lax.dot_general(qhead, ck[r], NT, preferred_element_type=F32) * score_scale
            score_own = lax.dot_general(qhead, own_bf, NT, preferred_element_type=F32) * score_scale
            score = jnp.where(live, score, mask_fill)
            score_own = jnp.where(mine_live, score_own, mask_fill)
            top = jnp.maximum(
                jnp.max(score, axis=1, keepdims=True), jnp.max(score_own, axis=1, keepdims=True)
            )
            weight = jnp.where(live, jnp.exp(score - top), 0.0)
            weight_own = jnp.where(mine_live, jnp.exp(score_own - top), 0.0)
            norm = jnp.sum(weight, axis=1, keepdims=True) + jnp.sum(
                weight_own, axis=1, keepdims=True
            )
            prob = (weight / norm).astype(BF16)
            prob_own = (weight_own / norm).astype(BF16)
            attended = jnp.dot(prob, cv[r], preferred_element_type=F32) + jnp.dot(
                prob_own, own_bf, preferred_element_type=F32
            )
            attended = jnp.sum(jnp.where(head_of, attended, 0.0), axis=0, keepdims=True)
            in_row, out_row = gates[r : r + 1, 0:NST], gates[r : r + 1, NST:]
            out_gate = jnp.broadcast_to(out_row, (NST, NST)).T
            in_gates.append(in_row)
            both_gates = jnp.sum(in_row * out_row, axis=1, keepdims=True)
            for j in range(HEADS):
                cols = slice(j * 128, (j + 1) * 128)
                seen = jnp.sum(out_gate * st[r, :, cols], axis=0, keepdims=True)
                mixed = (
                    attended[:, cols]
                    + decay[r : r + 1, cols] * seen
                    + both_gates * drive[r : r + 1, cols]
                )
                mixbuf[s, g, r : r + 1, cols] = mixed.astype(BF16).astype(F32)

        copies2 = [
            send(
                mixbuf.at[s, g], mixbuf.at[s, g],
                ms_s.at[s, d - 1], ms_r.at[s, d - 1], at_g(d),
            )
            for d in (1, 2, 3)
        ]
        for copy in copies2:
            copy.start()
        for r in range(2):
            in_gate = jnp.broadcast_to(in_gates[r], (NST, NST)).T
            for j in range(HEADS):
                cols = slice(j * 128, (j + 1) * 128)
                st[r, :, cols] = (
                    decay[r : r + 1, cols] * st[r, :, cols] + in_gate * drive[r : r + 1, cols]
                )
        for copy in copies2:
            copy.wait_recv()
        for i in range(4):
            mix8[2 * i : 2 * i + 2, :] = mixbuf[s, i]
        lhs = mix8[...].astype(BF16)
        copies3 = []
        for half in range(2):
            cbuf[s, half, tp] = jnp.dot(
                lhs, wblk[:, half * 640 : (half + 1) * 640], preferred_element_type=F32
            )
            for d in (1, 2, 3):
                place = cbuf.at[s, half, tp]
                sems = cs_s.at[s, half, d - 1], cs_r.at[s, half, d - 1]
                copies3.append(send(place, place, *sems, at_tp(d)))
                copies3[-1].start()
        for half in range(2):
            for copy in copies3[3 * half : 3 * half + 3]:
                copy.wait_recv()
            cols = slice(half * 640, (half + 1) * 640)
            hid[:, cols] = hid[:, cols] + (
                (cbuf[s, half, 0] + cbuf[s, half, 1]) + (cbuf[s, half, 2] + cbuf[s, half, 3])
            )
        for copy in copies + copies2 + copies3:
            copy.wait_send()
        return 0

    lax.fori_loop(0, STEPS, decode_step, 0)

    for i in range(4):
        fsrc[i] = hid[2 * i : 2 * i + 2, :]
    last = [
        go(send(fsrc.at[(g + d) % 4], fbuf.at[g], fs_s.at[d - 1], fs_r.at[d - 1], at_g(d)))
        for d in (1, 2, 3)
    ]
    fbuf[g] = fsrc[g]
    for copy in last:
        copy.wait_recv()
    for i in range(4):
        out_ref[:, i * BLK : (i + 1) * BLK] = fbuf[i].astype(BF16)
    store.wait()
    for copy in sent:
        copy.wait_send()


def on_device(
    learner_input, cotangent, token_ids, rewards, group_ids, weight_master, adam_first,
    adam_second, hidden_rows, cache_keys, cache_values, cache_lengths, ssm_state,
    state_weight, decay_rate,
):
    hbm = pl.BlockSpec(memory_space=pl.ANY)
    vmem = pl.BlockSpec(memory_space=pltpu.VMEM)
    smem = pl.BlockSpec(memory_space=pltpu.SMEM)
    dma = pltpu.SemaphoreType.DMA
    V = pltpu.VMEM
    shard = jax.ShapeDtypeStruct((SH, BLK), F32)
    rows = jax.ShapeDtypeStruct((2, D), BF16)
    grad, decoded = pl.pallas_call(
        kernel,
        out_shape=(shard, rows),
        in_specs=[hbm, hbm] + [vmem] * 3 + [hbm] * 3 + [vmem] + [hbm] * 2 + [smem] + [hbm] * 2 + [vmem],
        out_specs=(hbm, vmem),
        scratch_shapes=[
            V((TOK, BLK), BF16), V((TOK, BLK), BF16), V((BLK, TOK), BF16),
            V((4, 4, SH, BLK), BF16), V((BLK, BLK), BF16),
            V((CHUNKS, 6, 4, SH, HW), BF16), V((CHUNKS, 3, SH, CW), BF16),
            V((CHUNKS, 4, SH, CW), BF16),
            V((SH, BLK), F32), V((SH, BLK), F32), V((SH, BLK), F32), V((SH, BLK), F32),
            V((4, 2, BLK), F32), V((4, 2, BLK), F32),
            V((2, LC, BLK), BF16), V((2, LC, BLK), BF16), V((2, NST, BLK), F32),
            V((BLK, 2 * NST), BF16), V((1, BLK), F32),
            V((8, BLK), F32), V((2, 16, BLK), F32),
            V((STEPS, 4, 2, QW), F32), V((STEPS, 3, 2, QW), F32),
            V((STEPS, 4, 2, BLK), F32), V((8, BLK), F32),
            V((STEPS, 2, 4, 8, 640), F32), V((4, 2, BLK), F32), V((4, 2, BLK), F32),
            dma((10,)),
            dma((CHUNKS, 6)), dma((CHUNKS, 6)), dma((CHUNKS, 3)), dma((CHUNKS, 3)),
            dma((CHUNKS, 3)), dma((CHUNKS, 3)), dma((CHUNKS, 4)), dma((CHUNKS, 4)),
            dma((3,)), dma((3,)), dma((STEPS, 3)), dma((STEPS, 3)),
            dma((STEPS, 3)), dma((STEPS, 3)), dma((STEPS, 2, 3)), dma((STEPS, 2, 3)),
            dma((3,)), dma((3,)),
        ],
        compiler_params=pltpu.CompilerParams(
            collective_id=0, has_side_effects=True, vmem_limit_bytes=56 * 1024 * 1024
        ),
    )(
        learner_input, cotangent, token_ids.reshape(8, 128), rewards.reshape(1, 64),
        group_ids.reshape(1, 64), weight_master, adam_first, adam_second, hidden_rows,
        cache_keys, cache_values, cache_lengths, ssm_state, state_weight,
        decay_rate.reshape(HEADS, 128),
    )
    part = pl.BlockSpec((SH, BLK // 2), lambda i: (0, i))
    whole = pl.BlockSpec((2, D), lambda i: (0, 0))
    return pl.pallas_call(
        finish,
        grid=(2,),
        out_shape=(shard, shard, shard, rows),
        in_specs=[part] * 4 + [whole],
        out_specs=(part, part, part, whole),
    )(grad, weight_master, adam_first, adam_second, decoded)


def solution(mesh):
    in_specs = (
        P("fsdp", "grp"), P("fsdp", "tp"), P("fsdp"), P(), P(),
        P(("tp", "fsdp"), "grp"), P(("tp", "fsdp"), "grp"), P(("tp", "fsdp"), "grp"),
        P(("fsdp", "grp"), None), P(("fsdp", "grp"), None, "tp"),
        P(("fsdp", "grp"), None, "tp"), P(("fsdp", "grp")),
        P(("fsdp", "grp"), None, "tp"), P(), P("tp"),
    )
    out_specs = (
        P(("tp", "fsdp"), "grp"), P(("tp", "fsdp"), "grp"), P(("tp", "fsdp"), "grp"),
        P(("fsdp", "grp"), None),
    )
    return jax.shard_map(
        on_device, mesh=mesh, in_specs=in_specs, out_specs=out_specs, check_vma=False
    )
```

```python
import functools
import math

import jax
import jax.numpy as jnp
from jax import lax
from jax.experimental import pallas as pl
from jax.experimental.pallas import tpu as pltpu
from jax.sharding import PartitionSpec as P

F32 = jnp.float32
BF16 = jnp.bfloat16
MESH = pl.DeviceIdType.MESH

D = 5120
HEAD = 128
NST = 128
SEQ = 256
STEPS = 4
BLK = 1280
SH = 80
TOK = 1024
CW = 128
CHUNKS = BLK // CW
LAG = (0, 2, 4, 6, 8, 10, 12)
LC = 128
HEADS = BLK // HEAD
QW = BLK + 2 * NST + 128

beta_one = 0.9
beta_two = 0.95
learn_rate = 0.001
weight_decay = 0.1
adam_eps = 1e-08
adam_step = 10.0
norm_eps = 1e-05
mask_fill = -1e30

NT = (((1,), (1,)), ((), ()))


def adam_update(grad, master, first, second):
    first = beta_one * first + (1.0 - beta_one) * grad
    second = beta_two * second + (1.0 - beta_two) * grad * grad
    update = (
        first
        / (1.0 - beta_one**adam_step)
        / (jnp.sqrt(second / (1.0 - beta_two**adam_step)) + adam_eps)
    )
    return master - learn_rate * (update + weight_decay * master), first, second


def finish(grad, master, first, second, rows, nw, nf, ns, out):
    nw[...], nf[...], ns[...] = adam_update(grad[...], master[...], first[...], second[...])
    out[...] = rows[...]


def kernel(
    inp_h, cot_h, ids_ref, rew_ref, grp_ref,
    wm_h, m1_h, m2_h, hid_ref, ck_h, cv_h, len_ref, st_h, sw_h, dec_ref,
    gout_h, out_ref,
    inp, cot, sigt, grad, wblk, ry, rz, zacc,
    wm, m1, m2, gsum, hsrc, hbuf, ck, cv, st, sw, dec,
    hid, own, qsend, qrecv, mixbuf, mix8, cbuf, fsrc, fbuf,
    lsem, ysend, yrecv, zsend, zrecv, azs, azr, ays, ayr,
    hs_s, hs_r, qs_s, qs_r, ms_s, ms_r, cs_s, cs_r, fs_s, fs_r,
):
    fs = lax.axis_index("fsdp")
    g = lax.axis_index("grp")
    tp = lax.axis_index("tp")
    z, y = fs // 4, fs % 4

    def at_y(d):
        return {"fsdp": z * 4 + (y + d) % 4}

    def at_z(d):
        return {"fsdp": ((z + d) % 4) * 4 + y}

    def at_g(d):
        return {"grp": (g + d) % 4}

    def at_both(dg, dt):
        return {"grp": (g + dg) % 4, "tp": (tp + dt) % 4}

    def at_tp(d):
        return {"tp": (tp + d) % 4}

    def send(src, dst, ssem, rsem, where):
        return pltpu.make_async_remote_copy(
            src_ref=src, dst_ref=dst, send_sem=ssem, recv_sem=rsem,
            device_id=where, device_id_type=MESH,
        )

    loads = [
        pltpu.make_async_copy(cot_h, cot, lsem.at[0]),
        pltpu.make_async_copy(inp_h, inp, lsem.at[1]),
        pltpu.make_async_copy(wm_h, wm, lsem.at[2]),
        pltpu.make_async_copy(m1_h, m1, lsem.at[3]),
        pltpu.make_async_copy(m2_h, m2, lsem.at[4]),
        pltpu.make_async_copy(ck_h, ck, lsem.at[5]),
        pltpu.make_async_copy(cv_h, cv, lsem.at[6]),
        pltpu.make_async_copy(st_h, st, lsem.at[7]),
        pltpu.make_async_copy(
            sw_h.at[pl.ds(pl.multiple_of(g * BLK, BLK), BLK), :], sw, lsem.at[8]
        ),
    ]
    for copy in loads[:2]:
        copy.start()

    barrier = pltpu.get_barrier_semaphore()
    greeted = [at_y(1), at_y(3)] + [at(d) for at in (at_z, at_g, at_tp) for d in (1, 2, 3)]
    greeted += [at_both(dg, dt) for dg in (1, 2, 3) for dt in (1, 2, 3)]
    for where in greeted:
        pl.semaphore_signal(barrier, inc=1, device_id=where, device_id_type=MESH)

    diag = lax.broadcasted_iota(jnp.int32, (64, 64), 0) == lax.broadcasted_iota(
        jnp.int32, (64, 64), 1
    )
    ids_row = jnp.broadcast_to(grp_ref[...].astype(F32), (64, 64))
    rew_row = jnp.broadcast_to(rew_ref[...], (64, 64))
    ids_col = jnp.sum(jnp.where(diag, ids_row, 0.0), axis=1, keepdims=True)
    rew_col = jnp.sum(jnp.where(diag, rew_row, 0.0), axis=1, keepdims=True)
    same = (ids_row == ids_col).astype(F32)
    adv = rew_ref[...] - jnp.sum(same * rew_col, axis=0, keepdims=True) / jnp.sum(
        same, axis=0, keepdims=True
    )
    mine = lax.broadcasted_iota(jnp.int32, (8, 64), 1) == fs * 4 + (
        lax.broadcasted_iota(jnp.int32, (8, 64), 0) // 2
    )
    adv8 = jnp.sum(jnp.where(mine, jnp.broadcast_to(adv, (8, 64)), 0.0), axis=1, keepdims=True)
    tw = jnp.where(ids_ref[...] != 0, jnp.broadcast_to(adv8, (8, 128)), 0.0) / SEQ

    for i in range(4):
        hsrc[i] = hid_ref[:, i * BLK : (i + 1) * BLK].astype(F32)
    for j in range(HEADS):
        dec[0:1, j * 128 : (j + 1) * 128] = dec_ref[j : j + 1, :]
    own[...] = jnp.zeros_like(own)

    loads[0].wait()

    def turn(j, _):
        col = pl.multiple_of(j * 128, 128)
        for k in range(TOK // 128):
            part = cot[k * 128 : (k + 1) * 128, pl.ds(col, 128)].T
            sigt[pl.ds(col, 128), k * 128 : (k + 1) * 128] = (
                part.astype(F32) * tw[k : k + 1, :]
            ).astype(BF16)
        return 0

    lax.fori_loop(0, BLK // 128, turn, 0)
    loads[1].wait()
    for copy in loads[2:]:
        copy.start()

    def gradient_chunk(c):
        def rows(q, _):
            part = jnp.dot(
                sigt[pl.ds(pl.multiple_of(q * 320, 320), 320), :],
                inp[:, c * 256 : (c + 1) * 256],
                preferred_element_type=F32,
            )
            grad[q, :, :, c * 256 : (c + 1) * 256] = part.astype(BF16).reshape(4, SH, 256)
            return 0

        lax.fori_loop(0, 4, rows, 0)

    wview = wblk.reshape(4, 4, SH, BLK)
    sent = []

    def go(copy):
        copy.start()
        sent.append(copy)
        return copy

    F, B = 0, 2
    ylast, zlast, azlast, aylast = {}, {}, {}, {}

    def columns(c):
        return pl.ds(c * CW, CW)

    def own_part(c, block, side):
        return grad[side : side + 2, block, :, c * CW : (c + 1) * CW].astype(F32)

    def y_send(c, k, src, d):
        ylast[c, k] = go(send(src, ry.at[c, k], ysend.at[c, k], yrecv.at[c, k], at_y(d)))

    def reduce_a(c):
        if c % 2 == 0 and c > 0:
            gradient_chunk(c // 2)
        for k, block, side, d in ((0, 2, F, 1), (2, 2, B, 3), (1, 1, B, 1), (3, 3, F, 3)):
            y_send(c, k, grad.at[pl.ds(side, 2), (y + block) % 4, :, columns(c)], d)

    def reduce_b(c):
        for k, block, side, d in ((0, 1, F, 1), (2, 3, B, 3)):
            ylast[c, k].wait_recv()
            ry[c, k] = (ry[c, k].astype(F32) + own_part(c, (y + block) % 4, side)).astype(BF16)
            y_send(c, 4 + k // 2, ry.at[c, k], d)

    def reduce_z(c):
        for k, last, side in ((3, 4, F), (1, 5, B)):
            ylast[c, k].wait_recv()
            ylast[c, last].wait_recv()
            zacc[c, side : side + 2] = (
                own_part(c, y, side) + ry[c, k].astype(F32) + ry[c, last].astype(F32)
            ).astype(BF16)
        for d in (1, 2, 3):
            zlast[c, d] = go(
                send(
                    zacc.at[c, (z + d) % 4], rz.at[c, d - 1],
                    zsend.at[c, d - 1], zrecv.at[c, d - 1], at_z(d),
                )
            )

    started = []

    def adam(c):
        cols = slice(c * CW, (c + 1) * CW)
        total = zacc[c, z].astype(F32)
        for d in (1, 2, 3):
            zlast[c, d].wait_recv()
            total = total + rz[c, d - 1].astype(F32)
        if not started:
            for copy in loads[2:5]:
                copy.wait()
        started.append(c)
        gsum[:, cols] = total
        fresh = adam_update(total, wm[:, cols], m1[:, cols], m2[:, cols])[0]
        wblk[pl.ds(pl.multiple_of(fs * SH, 16), SH), cols] = fresh.astype(BF16)
        if len(started) == CHUNKS:
            store.start()
        place = wview.at[z, y, :, columns(c)]
        for d in (1, 2, 3):
            azlast[c, d] = go(send(place, place, azs.at[c, d - 1], azr.at[c, d - 1], at_z(d)))

    def gather_a(c):
        for d in (1, 2, 3):
            azlast[c, d].wait_recv()
        for k, d in ((0, 1), (1, 3)):
            place = wview.at[:, y, :, columns(c)]
            aylast[c, k] = go(send(place, place, ays.at[c, k], ayr.at[c, k], at_y(d)))

    def gather_b(c):
        for k, block, side, d in ((0, 3, F, 1), (1, 1, B, 3)):
            aylast[c, k].wait_recv()
            place = wview.at[pl.ds(side, 2), (y + block) % 4, :, columns(c)]
            aylast[c, k + 2] = go(
                send(place, place, ays.at[c, k + 2], ayr.at[c, k + 2], at_y(d))
            )

    def gather_end(c):
        aylast[c, 2].wait_recv()
        aylast[c, 3].wait_recv()

    stages = (reduce_a, reduce_b, reduce_z, adam, gather_a, gather_b, gather_end)
    store = pltpu.make_async_copy(gsum, gout_h, lsem.at[9])
    hcopies = [
        send(hsrc.at[(g + d) % 4], hbuf.at[g], hs_s.at[d - 1], hs_r.at[d - 1], at_g(d))
        for d in (1, 2, 3)
    ]
    gradient_chunk(0)
    pl.semaphore_wait(barrier, len(greeted))
    for t in range(LAG[-1] + CHUNKS):
        for stage, lag in zip(stages, LAG):
            if 0 <= t - lag < CHUNKS:
                stage(t - lag)
        if t == 0:
            for copy in hcopies:
                copy.start()
            hbuf[g] = hsrc[g]

    for copy in hcopies:
        copy.wait()
    for i in range(4):
        hid[2 * i : 2 * i + 2, :] = hbuf[i]
    for copy in loads[5:]:
        copy.wait()

    head_of = (
        lax.broadcasted_iota(jnp.int32, (16, BLK), 1) // HEAD
        == lax.broadcasted_iota(jnp.int32, (16, BLK), 0)
    )
    own_row = lax.broadcasted_iota(jnp.int32, (16, BLK), 0)
    place128 = lax.broadcasted_iota(jnp.int32, (16, LC), 1)
    place16 = lax.broadcasted_iota(jnp.int32, (16, 16), 1)
    score_scale = 1.0 / math.sqrt(HEAD)

    def tp_copies(s):
        return [
            send(
                cbuf.at[s, tp], cbuf.at[s, tp], cs_s.at[s, d - 1], cs_r.at[s, d - 1], at_tp(d)
            )
            for d in (2, 1, 3)
        ]

    def decode_step(s, _, last=False):
        h = hid[...]
        high = h.astype(BF16).astype(F32)
        both = jnp.concatenate([high, h - high], axis=0).astype(BF16)
        for n in range(BLK // 256):
            part = lax.dot_general(
                both, wblk[n * 256 : (n + 1) * 256, :], NT, preferred_element_type=F32
            )
            part = part[0:8] + part[8:16]
            for i in range(4):
                qsend[s, i, :, n * 256 : (n + 1) * 256] = part[2 * i : 2 * i + 2]
        part = jnp.dot(both, sw[...], preferred_element_type=F32)
        part = part[0:8] + part[8:16]
        square = jnp.broadcast_to(jnp.sum(h * h, axis=1, keepdims=True), (8, 128))
        for i in range(4):
            qsend[s, i, :, BLK : BLK + 2 * NST] = part[2 * i : 2 * i + 2]
            qsend[s, i, :, BLK + 2 * NST :] = square[2 * i : 2 * i + 2]
        copies = [
            send(
                qsend.at[s, (g + d) % 4], qrecv.at[s, d - 1],
                qs_s.at[s, d - 1], qs_r.at[s, d - 1], at_g(d),
            )
            for d in (1, 2, 3)
        ]
        for copy in copies:
            copy.start()
        total = qsend[s, g]
        for d, copy in enumerate(copies):
            copy.wait_recv()
            total = total + qrecv[s, d]
        scale = lax.rsqrt(total[:, BLK + 2 * NST : BLK + 2 * NST + 1] * (1.0 / D) + norm_eps)
        query = total[:, 0:BLK] * scale
        gates = total[:, BLK : BLK + 2 * NST] * scale
        query_bf = query.astype(BF16).astype(F32)
        step_size = jnp.maximum(query, 0.0) + jnp.log1p(jnp.exp(-jnp.abs(query)))
        decay = jnp.exp(-dec[...] * step_size)
        drive = step_size * query

        in_gates = []
        for r in range(2):
            qrow = jnp.broadcast_to(query_bf[r : r + 1, :], (16, BLK))
            own_now = jnp.where(own_row == s, qrow, own[r])
            own[r] = own_now
            own_bf = own_now.astype(BF16)
            qhead = jnp.where(head_of, qrow, 0.0).astype(BF16)
            live = place128 < len_ref[r]
            mine_live = place16 <= s
            score = lax.dot_general(qhead, ck[r], NT, preferred_element_type=F32) * score_scale
            score_own = lax.dot_general(qhead, own_bf, NT, preferred_element_type=F32) * score_scale
            score = jnp.where(live, score, mask_fill)
            score_own = jnp.where(mine_live, score_own, mask_fill)
            top = jnp.maximum(
                jnp.max(score, axis=1, keepdims=True), jnp.max(score_own, axis=1, keepdims=True)
            )
            weight = jnp.where(live, jnp.exp(score - top), 0.0)
            weight_own = jnp.where(mine_live, jnp.exp(score_own - top), 0.0)
            norm = jnp.sum(weight, axis=1, keepdims=True) + jnp.sum(
                weight_own, axis=1, keepdims=True
            )
            prob = (weight / norm).astype(BF16)
            prob_own = (weight_own / norm).astype(BF16)
            attended = jnp.dot(prob, cv[r], preferred_element_type=F32) + jnp.dot(
                prob_own, own_bf, preferred_element_type=F32
            )
            attended = jnp.sum(jnp.where(head_of, attended, 0.0), axis=0, keepdims=True)
            in_row, out_row = gates[r : r + 1, 0:NST], gates[r : r + 1, NST:]
            out_gate = jnp.broadcast_to(out_row, (NST, NST)).T
            in_gates.append(in_row)
            both_gates = jnp.sum(in_row * out_row, axis=1, keepdims=True)
            for j in range(HEADS):
                cols = slice(j * 128, (j + 1) * 128)
                seen = jnp.sum(out_gate * st[r, :, cols], axis=0, keepdims=True)
                mixed = (
                    attended[:, cols]
                    + decay[r : r + 1, cols] * seen
                    + both_gates * drive[r : r + 1, cols]
                )
                mixbuf[s, g, r : r + 1, cols] = mixed.astype(BF16).astype(F32)

        copies2 = [
            send(
                mixbuf.at[s, g], mixbuf.at[s, g],
                ms_s.at[s, d - 1], ms_r.at[s, d - 1], at_g(d),
            )
            for d in (1, 2, 3)
        ]
        for copy in copies2:
            copy.start()
        for copy in copies:
            copy.wait_send()
        for r in range(0 if last else 2):
            in_gate = jnp.broadcast_to(in_gates[r], (NST, NST)).T
            for j in range(HEADS):
                cols = slice(j * 128, (j + 1) * 128)
                st[r, :, cols] = (
                    decay[r : r + 1, cols] * st[r, :, cols] + in_gate * drive[r : r + 1, cols]
                )
        for copy in copies2:
            copy.wait_recv()
        for i in range(4):
            mix8[2 * i : 2 * i + 2, :] = mixbuf[s, i]
        lhs = mix8[...].astype(BF16)
        part = [
            jnp.dot(lhs, wblk[:, half * 640 : (half + 1) * 640], preferred_element_type=F32)
            for half in range(2)
        ]
        if last:
            return part, copies2
        cbuf[s, tp] = jnp.concatenate(part, axis=0).astype(BF16)
        copies3 = tp_copies(s)
        for copy in copies3:
            copy.start()
        for copy in copies2:
            copy.wait_send()
        for copy in copies3:
            copy.wait_recv()
        total = (cbuf[s, 0].astype(F32) + cbuf[s, 1].astype(F32)) + (
            cbuf[s, 2].astype(F32) + cbuf[s, 3].astype(F32)
        )
        hid[:, 0:640] = hid[:, 0:640] + total[0:8]
        hid[:, 640:] = hid[:, 640:] + total[8:16]
        return 0

    lax.fori_loop(0, STEPS - 1, decode_step, 0)
    part, pending = decode_step(STEPS - 1, 0, last=True)
    for half in range(2):
        cols = slice(half * 640, (half + 1) * 640)
        value = part[half] + jnp.where(tp == 0, hid[:, cols], 0.0)
        for i in range(4):
            fsrc[i, :, cols] = value[2 * i : 2 * i + 2]
    final = [
        send(
            fsrc.at[(g + dg) % 4], fbuf.at[g, tp],
            fs_s.at[dg, dt], fs_r.at[dg, dt], at_both(dg, dt),
        )
        for dg in (2, 1, 3, 0) for dt in (2, 3, 1, 0) if dg + dt > 0
    ]
    for copy in final:
        copy.start()
    fbuf[g, tp] = fsrc[g]
    store.wait()
    for copy in sent + pending:
        copy.wait_send()
    for s in range(STEPS - 1):
        for copy in tp_copies(s):
            copy.wait_send()
    for copy in final:
        copy.wait()
    for i in range(4):
        out_ref[:, i * BLK : (i + 1) * BLK] = (
            (fbuf[i, 0] + fbuf[i, 1]) + (fbuf[i, 2] + fbuf[i, 3])
        ).astype(BF16)


def on_device(
    learner_input, cotangent, token_ids, rewards, group_ids, weight_master, adam_first,
    adam_second, hidden_rows, cache_keys, cache_values, cache_lengths, ssm_state,
    state_weight, decay_rate,
):
    hbm = pl.BlockSpec(memory_space=pl.ANY)
    vmem = pl.BlockSpec(memory_space=pltpu.VMEM)
    smem = pl.BlockSpec(memory_space=pltpu.SMEM)
    dma = pltpu.SemaphoreType.DMA
    V = pltpu.VMEM
    shard = jax.ShapeDtypeStruct((SH, BLK), F32)
    rows = jax.ShapeDtypeStruct((2, D), BF16)
    grad, decoded = pl.pallas_call(
        kernel,
        out_shape=(shard, rows),
        in_specs=[hbm, hbm] + [vmem] * 3 + [hbm] * 3 + [vmem] + [hbm] * 2 + [smem] + [hbm] * 2 + [vmem],
        out_specs=(hbm, vmem),
        scratch_shapes=[
            V((TOK, BLK), BF16), V((TOK, BLK), BF16), V((BLK, TOK), BF16),
            V((4, 4, SH, BLK), BF16), V((BLK, BLK), BF16),
            V((CHUNKS, 6, 2, SH, CW), BF16), V((CHUNKS, 3, SH, CW), BF16),
            V((CHUNKS, 4, SH, CW), BF16),
            V((SH, BLK), F32), V((SH, BLK), F32), V((SH, BLK), F32), V((SH, BLK), F32),
            V((4, 2, BLK), F32), V((4, 2, BLK), F32),
            V((2, LC, BLK), BF16), V((2, LC, BLK), BF16), V((2, NST, BLK), F32),
            V((BLK, 2 * NST), BF16), V((1, BLK), F32),
            V((8, BLK), F32), V((2, 16, BLK), F32),
            V((STEPS, 4, 2, QW), F32), V((STEPS, 3, 2, QW), F32),
            V((STEPS, 4, 2, BLK), F32), V((8, BLK), F32),
            V((STEPS, 4, 16, 640), BF16), V((4, 2, BLK), F32), V((4, 4, 2, BLK), F32),
            dma((10,)),
            dma((CHUNKS, 6)), dma((CHUNKS, 6)), dma((CHUNKS, 3)), dma((CHUNKS, 3)),
            dma((CHUNKS, 3)), dma((CHUNKS, 3)), dma((CHUNKS, 4)), dma((CHUNKS, 4)),
            dma((3,)), dma((3,)), dma((STEPS, 3)), dma((STEPS, 3)),
            dma((STEPS, 3)), dma((STEPS, 3)), dma((STEPS, 3)), dma((STEPS, 3)),
            dma((4, 4)), dma((4, 4)),
        ],
        compiler_params=pltpu.CompilerParams(
            collective_id=0, has_side_effects=True, vmem_limit_bytes=56 * 1024 * 1024
        ),
    )(
        learner_input, cotangent, token_ids.reshape(8, 128), rewards.reshape(1, 64),
        group_ids.reshape(1, 64), weight_master, adam_first, adam_second, hidden_rows,
        cache_keys, cache_values, cache_lengths, ssm_state, state_weight,
        decay_rate.reshape(HEADS, 128),
    )
    part = pl.BlockSpec((SH, BLK // 2), lambda i: (0, i))
    whole = pl.BlockSpec((2, D), lambda i: (0, 0))
    return pl.pallas_call(
        finish,
        grid=(2,),
        out_shape=(shard, shard, shard, rows),
        in_specs=[part] * 4 + [whole],
        out_specs=(part, part, part, whole),
    )(grad, weight_master, adam_first, adam_second, decoded)


def solution(mesh):
    in_specs = (
        P("fsdp", "grp"), P("fsdp", "tp"), P("fsdp"), P(), P(),
        P(("tp", "fsdp"), "grp"), P(("tp", "fsdp"), "grp"), P(("tp", "fsdp"), "grp"),
        P(("fsdp", "grp"), None), P(("fsdp", "grp"), None, "tp"),
        P(("fsdp", "grp"), None, "tp"), P(("fsdp", "grp")),
        P(("fsdp", "grp"), None, "tp"), P(), P("tp"),
    )
    out_specs = (
        P(("tp", "fsdp"), "grp"), P(("tp", "fsdp"), "grp"), P(("tp", "fsdp"), "grp"),
        P(("fsdp", "grp"), None),
    )
    return jax.shard_map(
        on_device, mesh=mesh, in_specs=in_specs, out_specs=out_specs, check_vma=False
    )
```

```python
import functools
import math

import jax
import jax.numpy as jnp
from jax import lax
from jax.experimental import pallas as pl
from jax.experimental.pallas import tpu as pltpu
from jax.sharding import PartitionSpec as P

F32 = jnp.float32
BF16 = jnp.bfloat16
MESH = pl.DeviceIdType.MESH

D = 5120
HEAD = 128
NST = 128
SEQ = 256
STEPS = 4
BLK = 1280
SH = 80
TOK = 1024
CW = 128
CHUNKS = BLK // CW
LAG = (0, 2, 4, 6, 8, 10, 12)
LC = 128
HEADS = BLK // HEAD
QW = BLK + 2 * NST + 128

beta_one = 0.9
beta_two = 0.95
learn_rate = 0.001
weight_decay = 0.1
adam_eps = 1e-08
adam_step = 10.0
norm_eps = 1e-05
mask_fill = -1e30

NT = (((1,), (1,)), ((), ()))


def adam_update(grad, master, first, second):
    first = beta_one * first + (1.0 - beta_one) * grad
    second = beta_two * second + (1.0 - beta_two) * grad * grad
    update = (
        first
        / (1.0 - beta_one**adam_step)
        / (jnp.sqrt(second / (1.0 - beta_two**adam_step)) + adam_eps)
    )
    return master - learn_rate * (update + weight_decay * master), first, second


def finish(grad, master, first, second, rows, nw, nf, ns, out):
    nw[...], nf[...], ns[...] = adam_update(grad[...], master[...], first[...], second[...])
    out[...] = rows[...]


def kernel(
    inp_h, cot_h, ids_ref, rew_ref, grp_ref,
    wm_h, m1_h, m2_h, hid_ref, ck_h, cv_h, len_ref, st_h, sw_h, dec_ref,
    gout_h, out_ref,
    inp, cot, sigt, grad, wblk, ry, rz, zacc,
    wm, m1, m2, gsum, hsrc, hbuf, ck, cv, st, sw, dec,
    hid, own, qsend, qrecv, mixbuf, mix8, cbuf, fsrc, fbuf,
    lsem, ysend, yrecv, zsend, zrecv, azs, azr, ays, ayr,
    hs_s, hs_r, qs_s, qs_r, ms_s, ms_r, cs_s, cs_r, fs_s, fs_r,
):
    fs = lax.axis_index("fsdp")
    g = lax.axis_index("grp")
    tp = lax.axis_index("tp")
    z, y = fs // 4, fs % 4

    y_ids = [(z * 4 + (y + d) % 4, g, tp) for d in range(4)]
    z_ids = [(((z + d) % 4) * 4 + y, g, tp) for d in range(4)]
    g_at = [(g + d) % 4 for d in range(4)]
    tp_at = [(tp + d) % 4 for d in range(4)]

    def at_y(d):
        return y_ids[d]

    def at_z(d):
        return z_ids[d]

    def at_g(d):
        return fs, g_at[d], tp

    def at_tp(d):
        return fs, g, tp_at[d]

    def at_both(dg, dt):
        return fs, g_at[dg], tp_at[dt]

    def send(src, dst, ssem, rsem, where):
        return pltpu.make_async_remote_copy(
            src_ref=src, dst_ref=dst, send_sem=ssem, recv_sem=rsem,
            device_id=where, device_id_type=MESH,
        )

    loads = [
        pltpu.make_async_copy(cot_h, cot, lsem.at[0]),
        pltpu.make_async_copy(inp_h, inp, lsem.at[1]),
        pltpu.make_async_copy(wm_h, wm, lsem.at[2]),
        pltpu.make_async_copy(m1_h, m1, lsem.at[3]),
        pltpu.make_async_copy(m2_h, m2, lsem.at[4]),
        pltpu.make_async_copy(ck_h, ck, lsem.at[5]),
        pltpu.make_async_copy(cv_h, cv, lsem.at[6]),
        pltpu.make_async_copy(st_h, st, lsem.at[7]),
        pltpu.make_async_copy(
            sw_h.at[pl.ds(pl.multiple_of(g * BLK, BLK), BLK), :], sw, lsem.at[8]
        ),
    ]
    for copy in loads[:2]:
        copy.start()

    barrier = pltpu.get_barrier_semaphore()
    greeted = [at_y(1), at_y(3)] + [at(d) for at in (at_z, at_g, at_tp) for d in (1, 2, 3)]
    greeted += [at_both(dg, dt) for dg in (1, 2, 3) for dt in (1, 2, 3)]
    for where in greeted:
        pl.semaphore_signal(barrier, inc=1, device_id=where, device_id_type=MESH)

    diag = lax.broadcasted_iota(jnp.int32, (64, 64), 0) == lax.broadcasted_iota(
        jnp.int32, (64, 64), 1
    )
    ids_row = jnp.broadcast_to(grp_ref[...].astype(F32), (64, 64))
    rew_row = jnp.broadcast_to(rew_ref[...], (64, 64))
    ids_col = jnp.sum(jnp.where(diag, ids_row, 0.0), axis=1, keepdims=True)
    rew_col = jnp.sum(jnp.where(diag, rew_row, 0.0), axis=1, keepdims=True)
    same = (ids_row == ids_col).astype(F32)
    adv = rew_ref[...] - jnp.sum(same * rew_col, axis=0, keepdims=True) / jnp.sum(
        same, axis=0, keepdims=True
    )
    mine = lax.broadcasted_iota(jnp.int32, (8, 64), 1) == fs * 4 + (
        lax.broadcasted_iota(jnp.int32, (8, 64), 0) // 2
    )
    adv8 = jnp.sum(jnp.where(mine, jnp.broadcast_to(adv, (8, 64)), 0.0), axis=1, keepdims=True)
    tw = jnp.where(ids_ref[...] != 0, jnp.broadcast_to(adv8, (8, 128)), 0.0) / SEQ

    for i in range(4):
        hsrc[i] = hid_ref[:, i * BLK : (i + 1) * BLK].astype(F32)
    for j in range(HEADS):
        dec[0:1, j * 128 : (j + 1) * 128] = dec_ref[j : j + 1, :]
    own[...] = jnp.zeros_like(own)

    loads[0].wait()

    def turn(j, _):
        col = pl.multiple_of(j * 128, 128)
        for k in range(TOK // 128):
            part = cot[k * 128 : (k + 1) * 128, pl.ds(col, 128)].T
            sigt[pl.ds(col, 128), k * 128 : (k + 1) * 128] = (
                part.astype(F32) * tw[k : k + 1, :]
            ).astype(BF16)
        return 0

    lax.fori_loop(0, BLK // 128, turn, 0)
    loads[1].wait()
    for copy in loads[2:]:
        copy.start()

    def gradient_chunk(c):
        def rows(q, _):
            part = jnp.dot(
                sigt[pl.ds(pl.multiple_of(q * 320, 320), 320), :],
                inp[:, c * 256 : (c + 1) * 256],
                preferred_element_type=F32,
            )
            grad[q, :, :, c * 256 : (c + 1) * 256] = part.astype(BF16).reshape(4, SH, 256)
            return 0

        lax.fori_loop(0, 4, rows, 0)

    wview = wblk.reshape(4, 4, SH, BLK)
    sent = []

    def go(copy):
        copy.start()
        sent.append(copy)
        return copy

    F, B = 0, 2
    ylast, zlast, azlast, aylast = {}, {}, {}, {}

    def columns(c):
        return pl.ds(c * CW, CW)

    def own_part(c, block, side):
        return grad[side : side + 2, block, :, c * CW : (c + 1) * CW].astype(F32)

    def y_send(c, k, src, d):
        ylast[c, k] = go(send(src, ry.at[c, k], ysend.at[c, k], yrecv.at[c, k], at_y(d)))

    def reduce_a(c):
        if c % 2 == 0 and c > 0:
            gradient_chunk(c // 2)
        for k, block, side, d in ((0, 2, F, 1), (2, 2, B, 3), (1, 1, B, 1), (3, 3, F, 3)):
            y_send(c, k, grad.at[pl.ds(side, 2), (y + block) % 4, :, columns(c)], d)

    def reduce_b(c):
        for k, block, side, d in ((0, 1, F, 1), (2, 3, B, 3)):
            ylast[c, k].wait_recv()
            ry[c, k] = (ry[c, k].astype(F32) + own_part(c, (y + block) % 4, side)).astype(BF16)
            y_send(c, 4 + k // 2, ry.at[c, k], d)

    def reduce_z(c):
        for k, last, side in ((3, 4, F), (1, 5, B)):
            ylast[c, k].wait_recv()
            ylast[c, last].wait_recv()
            zacc[c, side : side + 2] = (
                own_part(c, y, side) + ry[c, k].astype(F32) + ry[c, last].astype(F32)
            ).astype(BF16)
        for d in (1, 2, 3):
            zlast[c, d] = go(
                send(
                    zacc.at[c, (z + d) % 4], rz.at[c, d - 1],
                    zsend.at[c, d - 1], zrecv.at[c, d - 1], at_z(d),
                )
            )

    started = []

    def adam(c):
        cols = slice(c * CW, (c + 1) * CW)
        total = zacc[c, z].astype(F32)
        for d in (1, 2, 3):
            zlast[c, d].wait_recv()
            total = total + rz[c, d - 1].astype(F32)
        if not started:
            for copy in loads[2:5]:
                copy.wait()
        started.append(c)
        gsum[:, cols] = total
        fresh = adam_update(total, wm[:, cols], m1[:, cols], m2[:, cols])[0]
        wblk[pl.ds(pl.multiple_of(fs * SH, 16), SH), cols] = fresh.astype(BF16)
        if len(started) == CHUNKS:
            store.start()
        place = wview.at[z, y, :, columns(c)]
        for d in (1, 2, 3):
            azlast[c, d] = go(send(place, place, azs.at[c, d - 1], azr.at[c, d - 1], at_z(d)))

    def gather_a(c):
        for d in (1, 2, 3):
            azlast[c, d].wait_recv()
        for k, d in ((0, 1), (1, 3)):
            place = wview.at[:, y, :, columns(c)]
            aylast[c, k] = go(send(place, place, ays.at[c, k], ayr.at[c, k], at_y(d)))

    def gather_b(c):
        for k, block, side, d in ((0, 3, F, 1), (1, 1, B, 3)):
            aylast[c, k].wait_recv()
            place = wview.at[pl.ds(side, 2), (y + block) % 4, :, columns(c)]
            aylast[c, k + 2] = go(
                send(place, place, ays.at[c, k + 2], ayr.at[c, k + 2], at_y(d))
            )

    def gather_end(c):
        aylast[c, 2].wait_recv()
        aylast[c, 3].wait_recv()

    stages = (reduce_a, reduce_b, reduce_z, adam, gather_a, gather_b, gather_end)
    store = pltpu.make_async_copy(gsum, gout_h, lsem.at[9])
    hcopies = [
        send(hsrc.at[(g + d) % 4], hbuf.at[g], hs_s.at[d - 1], hs_r.at[d - 1], at_g(d))
        for d in (1, 2, 3)
    ]
    gradient_chunk(0)
    pl.semaphore_wait(barrier, len(greeted))
    for t in range(LAG[-1] + CHUNKS):
        for stage, lag in list(zip(stages, LAG))[1:] + [(reduce_a, 0)]:
            if 0 <= t - lag < CHUNKS:
                stage(t - lag)
        if t == 0:
            for copy in hcopies:
                copy.start()
            hbuf[g] = hsrc[g]

    for copy in hcopies:
        copy.wait()
    for i in range(4):
        hid[2 * i : 2 * i + 2, :] = hbuf[i]
    for copy in loads[5:]:
        copy.wait()

    head_of = (
        lax.broadcasted_iota(jnp.int32, (16, BLK), 1) // HEAD
        == lax.broadcasted_iota(jnp.int32, (16, BLK), 0)
    )
    own_row = lax.broadcasted_iota(jnp.int32, (16, BLK), 0)
    place128 = lax.broadcasted_iota(jnp.int32, (16, LC), 1)
    place16 = lax.broadcasted_iota(jnp.int32, (16, 16), 1)
    score_scale = 1.0 / math.sqrt(HEAD)

    def tp_copies(s):
        return [
            send(
                cbuf.at[s, tp], cbuf.at[s, tp], cs_s.at[s, d - 1], cs_r.at[s, d - 1], at_tp(d)
            )
            for d in (2, 1, 3)
        ]

    def decode_step(s, _, last=False):
        h = hid[...]
        high = h.astype(BF16).astype(F32)
        both = jnp.concatenate([high, h - high], axis=0).astype(BF16)
        for n in range(BLK // 256):
            part = lax.dot_general(
                both, wblk[n * 256 : (n + 1) * 256, :], NT, preferred_element_type=F32
            )
            part = part[0:8] + part[8:16]
            for i in range(4):
                qsend[s, i, :, n * 256 : (n + 1) * 256] = part[2 * i : 2 * i + 2]
        part = jnp.dot(both, sw[...], preferred_element_type=F32)
        part = part[0:8] + part[8:16]
        square = jnp.broadcast_to(jnp.sum(h * h, axis=1, keepdims=True), (8, 128))
        for i in range(4):
            qsend[s, i, :, BLK : BLK + 2 * NST] = part[2 * i : 2 * i + 2]
            qsend[s, i, :, BLK + 2 * NST :] = square[2 * i : 2 * i + 2]
        copies = [
            send(
                qsend.at[s, (g + d) % 4], qrecv.at[s, d - 1],
                qs_s.at[s, d - 1], qs_r.at[s, d - 1], at_g(d),
            )
            for d in (1, 2, 3)
        ]
        for copy in copies:
            copy.start()
        total = qsend[s, g]
        for d, copy in enumerate(copies):
            copy.wait_recv()
            total = total + qrecv[s, d]
        scale = lax.rsqrt(total[:, BLK + 2 * NST : BLK + 2 * NST + 1] * (1.0 / D) + norm_eps)
        query = total[:, 0:BLK] * scale
        gates = total[:, BLK : BLK + 2 * NST] * scale
        query_bf = query.astype(BF16).astype(F32)
        step_size = jnp.maximum(query, 0.0) + jnp.log1p(jnp.exp(-jnp.abs(query)))
        decay = jnp.exp(-dec[...] * step_size)
        drive = step_size * query

        in_gates = []
        for r in range(2):
            qrow = jnp.broadcast_to(query_bf[r : r + 1, :], (16, BLK))
            own_now = jnp.where(own_row == s, qrow, own[r])
            own[r] = own_now
            own_bf = own_now.astype(BF16)
            qhead = jnp.where(head_of, qrow, 0.0).astype(BF16)
            live = place128 < len_ref[r]
            mine_live = place16 <= s
            score = lax.dot_general(qhead, ck[r], NT, preferred_element_type=F32) * score_scale
            score_own = lax.dot_general(qhead, own_bf, NT, preferred_element_type=F32) * score_scale
            score = jnp.where(live, score, mask_fill)
            score_own = jnp.where(mine_live, score_own, mask_fill)
            top = jnp.maximum(
                jnp.max(score, axis=1, keepdims=True), jnp.max(score_own, axis=1, keepdims=True)
            )
            weight = jnp.where(live, jnp.exp(score - top), 0.0)
            weight_own = jnp.where(mine_live, jnp.exp(score_own - top), 0.0)
            norm = jnp.sum(weight, axis=1, keepdims=True) + jnp.sum(
                weight_own, axis=1, keepdims=True
            )
            prob = (weight / norm).astype(BF16)
            prob_own = (weight_own / norm).astype(BF16)
            attended = jnp.dot(prob, cv[r], preferred_element_type=F32) + jnp.dot(
                prob_own, own_bf, preferred_element_type=F32
            )
            attended = jnp.sum(jnp.where(head_of, attended, 0.0), axis=0, keepdims=True)
            in_row, out_row = gates[r : r + 1, 0:NST], gates[r : r + 1, NST:]
            out_gate = jnp.broadcast_to(out_row, (NST, NST)).T
            in_gates.append(in_row)
            both_gates = jnp.sum(in_row * out_row, axis=1, keepdims=True)
            for j in range(HEADS):
                cols = slice(j * 128, (j + 1) * 128)
                seen = jnp.sum(out_gate * st[r, :, cols], axis=0, keepdims=True)
                mixed = (
                    attended[:, cols]
                    + decay[r : r + 1, cols] * seen
                    + both_gates * drive[r : r + 1, cols]
                )
                mixbuf[s, g, r : r + 1, cols] = mixed.astype(BF16).astype(F32)

        copies2 = [
            send(
                mixbuf.at[s, g], mixbuf.at[s, g],
                ms_s.at[s, d - 1], ms_r.at[s, d - 1], at_g(d),
            )
            for d in (1, 2, 3)
        ]
        for copy in copies2:
            copy.start()
        for copy in copies:
            copy.wait_send()
        for r in range(0 if last else 2):
            in_gate = jnp.broadcast_to(in_gates[r], (NST, NST)).T
            for j in range(HEADS):
                cols = slice(j * 128, (j + 1) * 128)
                st[r, :, cols] = (
                    decay[r : r + 1, cols] * st[r, :, cols] + in_gate * drive[r : r + 1, cols]
                )
        for copy in copies2:
            copy.wait_recv()
        for i in range(4):
            mix8[2 * i : 2 * i + 2, :] = mixbuf[s, i]
        lhs = mix8[...].astype(BF16)
        part = [
            jnp.dot(lhs, wblk[:, half * 640 : (half + 1) * 640], preferred_element_type=F32)
            for half in range(2)
        ]
        if last:
            return part, copies2
        cbuf[s, tp] = jnp.concatenate(part, axis=0).astype(BF16)
        copies3 = tp_copies(s)
        for copy in copies3:
            copy.start()
        for copy in copies2:
            copy.wait_send()
        for copy in copies3:
            copy.wait_recv()
        total = (cbuf[s, 0].astype(F32) + cbuf[s, 1].astype(F32)) + (
            cbuf[s, 2].astype(F32) + cbuf[s, 3].astype(F32)
        )
        hid[:, 0:640] = hid[:, 0:640] + total[0:8]
        hid[:, 640:] = hid[:, 640:] + total[8:16]
        return 0

    lax.fori_loop(0, STEPS - 1, decode_step, 0)
    part, pending = decode_step(STEPS - 1, 0, last=True)
    for half in range(2):
        cols = slice(half * 640, (half + 1) * 640)
        value = part[half] + jnp.where(tp == 0, hid[:, cols], 0.0)
        for i in range(4):
            fsrc[i, :, cols] = value[2 * i : 2 * i + 2]
    final = [
        send(
            fsrc.at[(g + dg) % 4], fbuf.at[g, tp],
            fs_s.at[dg, dt], fs_r.at[dg, dt], at_both(dg, dt),
        )
        for dg in (2, 1, 3, 0) for dt in (2, 3, 1, 0) if dg + dt > 0
    ]
    for copy in final:
        copy.start()
    fbuf[g, tp] = fsrc[g]
    store.wait()
    for copy in sent + pending:
        copy.wait_send()
    for s in range(STEPS - 1):
        for copy in tp_copies(s):
            copy.wait_send()
    for copy in final:
        copy.wait()
    for i in range(4):
        out_ref[:, i * BLK : (i + 1) * BLK] = (
            (fbuf[i, 0] + fbuf[i, 1]) + (fbuf[i, 2] + fbuf[i, 3])
        ).astype(BF16)


def on_device(
    learner_input, cotangent, token_ids, rewards, group_ids, weight_master, adam_first,
    adam_second, hidden_rows, cache_keys, cache_values, cache_lengths, ssm_state,
    state_weight, decay_rate,
):
    hbm = pl.BlockSpec(memory_space=pl.ANY)
    vmem = pl.BlockSpec(memory_space=pltpu.VMEM)
    smem = pl.BlockSpec(memory_space=pltpu.SMEM)
    dma = pltpu.SemaphoreType.DMA
    V = pltpu.VMEM
    shard = jax.ShapeDtypeStruct((SH, BLK), F32)
    rows = jax.ShapeDtypeStruct((2, D), BF16)
    grad, decoded = pl.pallas_call(
        kernel,
        out_shape=(shard, rows),
        in_specs=[hbm, hbm] + [vmem] * 3 + [hbm] * 3 + [vmem] + [hbm] * 2 + [smem] + [hbm] * 2 + [vmem],
        out_specs=(hbm, vmem),
        scratch_shapes=[
            V((TOK, BLK), BF16), V((TOK, BLK), BF16), V((BLK, TOK), BF16),
            V((4, 4, SH, BLK), BF16), V((BLK, BLK), BF16),
            V((CHUNKS, 6, 2, SH, CW), BF16), V((CHUNKS, 3, SH, CW), BF16),
            V((CHUNKS, 4, SH, CW), BF16),
            V((SH, BLK), F32), V((SH, BLK), F32), V((SH, BLK), F32), V((SH, BLK), F32),
            V((4, 2, BLK), F32), V((4, 2, BLK), F32),
            V((2, LC, BLK), BF16), V((2, LC, BLK), BF16), V((2, NST, BLK), F32),
            V((BLK, 2 * NST), BF16), V((1, BLK), F32),
            V((8, BLK), F32), V((2, 16, BLK), F32),
            V((STEPS, 4, 2, QW), F32), V((STEPS, 3, 2, QW), F32),
            V((STEPS, 4, 2, BLK), F32), V((8, BLK), F32),
            V((STEPS, 4, 16, 640), BF16), V((4, 2, BLK), F32), V((4, 4, 2, BLK), F32),
            dma((10,)),
            dma((CHUNKS, 6)), dma((CHUNKS, 6)), dma((CHUNKS, 3)), dma((CHUNKS, 3)),
            dma((CHUNKS, 3)), dma((CHUNKS, 3)), dma((CHUNKS, 4)), dma((CHUNKS, 4)),
            dma((3,)), dma((3,)), dma((STEPS, 3)), dma((STEPS, 3)),
            dma((STEPS, 3)), dma((STEPS, 3)), dma((STEPS, 3)), dma((STEPS, 3)),
            dma((4, 4)), dma((4, 4)),
        ],
        compiler_params=pltpu.CompilerParams(
            collective_id=0, has_side_effects=True, vmem_limit_bytes=56 * 1024 * 1024
        ),
    )(
        learner_input, cotangent, token_ids.reshape(8, 128), rewards.reshape(1, 64),
        group_ids.reshape(1, 64), weight_master, adam_first, adam_second, hidden_rows,
        cache_keys, cache_values, cache_lengths, ssm_state, state_weight,
        decay_rate.reshape(HEADS, 128),
    )
    part = pl.BlockSpec((SH, BLK // 2), lambda i: (0, i))
    whole = pl.BlockSpec((2, D), lambda i: (0, 0))
    return pl.pallas_call(
        finish,
        grid=(2,),
        out_shape=(shard, shard, shard, rows),
        in_specs=[part] * 4 + [whole],
        out_specs=(part, part, part, whole),
    )(grad, weight_master, adam_first, adam_second, decoded)


def solution(mesh):
    in_specs = (
        P("fsdp", "grp"), P("fsdp", "tp"), P("fsdp"), P(), P(),
        P(("tp", "fsdp"), "grp"), P(("tp", "fsdp"), "grp"), P(("tp", "fsdp"), "grp"),
        P(("fsdp", "grp"), None), P(("fsdp", "grp"), None, "tp"),
        P(("fsdp", "grp"), None, "tp"), P(("fsdp", "grp")),
        P(("fsdp", "grp"), None, "tp"), P(), P("tp"),
    )
    out_specs = (
        P(("tp", "fsdp"), "grp"), P(("tp", "fsdp"), "grp"), P(("tp", "fsdp"), "grp"),
        P(("fsdp", "grp"), None),
    )
    return jax.shard_map(
        on_device, mesh=mesh, in_specs=in_specs, out_specs=out_specs, check_vma=False
    )
```

```python
import functools
import math

import jax
import jax.numpy as jnp
from jax import lax
from jax.experimental import pallas as pl
from jax.experimental.pallas import tpu as pltpu
from jax.sharding import PartitionSpec as P

F32 = jnp.float32
BF16 = jnp.bfloat16
MESH = pl.DeviceIdType.MESH

D = 5120
HEAD = 128
NST = 128
SEQ = 256
STEPS = 4
BLK = 1280
SH = 80
TOK = 1024
CW = 128
CHUNKS = BLK // CW
EARLY = BLK - 2 * CW
LAG = (0, 2, 4, 6, 8, 10, 12)
LC = 128
HEADS = BLK // HEAD
QW = BLK + 2 * NST + 128

beta_one = 0.9
beta_two = 0.95
learn_rate = 0.001
weight_decay = 0.1
adam_eps = 1e-08
adam_step = 10.0
norm_eps = 1e-05
mask_fill = -1e30

NT = (((1,), (1,)), ((), ()))


def adam_update(grad, master, first, second):
    first = beta_one * first + (1.0 - beta_one) * grad
    second = beta_two * second + (1.0 - beta_two) * grad * grad
    update = (
        first
        / (1.0 - beta_one**adam_step)
        / (jnp.sqrt(second / (1.0 - beta_two**adam_step)) + adam_eps)
    )
    return master - learn_rate * (update + weight_decay * master), first, second


def finish(grad, master, first, second, rows, nw, nf, ns, out):
    nw[...], nf[...], ns[...] = adam_update(grad[...], master[...], first[...], second[...])
    out[...] = rows[...]


def kernel(
    inp_h, cot_h, ids_ref, rew_ref, grp_ref,
    wm_h, m1_h, m2_h, hid_ref, ck_h, cv_h, len_ref, st_h, sw_h, dec_ref,
    gout_h, out_ref,
    inp, cot, sigt, grad, wblk, ry, rz, zacc,
    wm, m1, m2, gsum, hsrc, hbuf, ck, cv, st, sw, dec,
    hid, qacc, own, qsend, qrecv, mixbuf, mix8, cbuf, fsrc, fbuf,
    lsem, ysend, yrecv, zsend, zrecv, azs, azr, ays, ayr,
    hs_s, hs_r, qs_s, qs_r, ms_s, ms_r, cs_s, cs_r, fs_s, fs_r,
):
    fs = lax.axis_index("fsdp")
    g = lax.axis_index("grp")
    tp = lax.axis_index("tp")
    z, y = fs // 4, fs % 4

    y_ids = [(z * 4 + (y + d) % 4, g, tp) for d in range(4)]
    z_ids = [(((z + d) % 4) * 4 + y, g, tp) for d in range(4)]
    g_at = [(g + d) % 4 for d in range(4)]
    tp_at = [(tp + d) % 4 for d in range(4)]

    def at_y(d):
        return y_ids[d]

    def at_z(d):
        return z_ids[d]

    def at_g(d):
        return fs, g_at[d], tp

    def at_tp(d):
        return fs, g, tp_at[d]

    def at_both(dg, dt):
        return fs, g_at[dg], tp_at[dt]

    def send(src, dst, ssem, rsem, where):
        return pltpu.make_async_remote_copy(
            src_ref=src, dst_ref=dst, send_sem=ssem, recv_sem=rsem,
            device_id=where, device_id_type=MESH,
        )

    loads = [
        pltpu.make_async_copy(cot_h, cot, lsem.at[0]),
        pltpu.make_async_copy(inp_h, inp, lsem.at[1]),
        pltpu.make_async_copy(wm_h, wm, lsem.at[2]),
        pltpu.make_async_copy(m1_h, m1, lsem.at[3]),
        pltpu.make_async_copy(m2_h, m2, lsem.at[4]),
        pltpu.make_async_copy(ck_h, ck, lsem.at[5]),
        pltpu.make_async_copy(cv_h, cv, lsem.at[6]),
        pltpu.make_async_copy(st_h, st, lsem.at[7]),
        pltpu.make_async_copy(
            sw_h.at[pl.ds(pl.multiple_of(g * BLK, BLK), BLK), :], sw, lsem.at[8]
        ),
    ]
    for copy in loads[:2]:
        copy.start()

    barrier = pltpu.get_barrier_semaphore()
    greeted = [at_y(1), at_y(3)] + [at(d) for at in (at_z, at_g, at_tp) for d in (1, 2, 3)]
    greeted += [at_both(dg, dt) for dg in (1, 2, 3) for dt in (1, 2, 3)]
    for where in greeted:
        pl.semaphore_signal(barrier, inc=1, device_id=where, device_id_type=MESH)

    diag = lax.broadcasted_iota(jnp.int32, (64, 64), 0) == lax.broadcasted_iota(
        jnp.int32, (64, 64), 1
    )
    ids_row = jnp.broadcast_to(grp_ref[...].astype(F32), (64, 64))
    rew_row = jnp.broadcast_to(rew_ref[...], (64, 64))
    ids_col = jnp.sum(jnp.where(diag, ids_row, 0.0), axis=1, keepdims=True)
    rew_col = jnp.sum(jnp.where(diag, rew_row, 0.0), axis=1, keepdims=True)
    same = (ids_row == ids_col).astype(F32)
    adv = rew_ref[...] - jnp.sum(same * rew_col, axis=0, keepdims=True) / jnp.sum(
        same, axis=0, keepdims=True
    )
    mine = lax.broadcasted_iota(jnp.int32, (8, 64), 1) == fs * 4 + (
        lax.broadcasted_iota(jnp.int32, (8, 64), 0) // 2
    )
    adv8 = jnp.sum(jnp.where(mine, jnp.broadcast_to(adv, (8, 64)), 0.0), axis=1, keepdims=True)
    tw = jnp.where(ids_ref[...] != 0, jnp.broadcast_to(adv8, (8, 128)), 0.0) / SEQ

    for i in range(4):
        hsrc[i] = hid_ref[:, i * BLK : (i + 1) * BLK].astype(F32)
    for j in range(HEADS):
        dec[0:1, j * 128 : (j + 1) * 128] = dec_ref[j : j + 1, :]
    own[...] = jnp.zeros_like(own)

    loads[0].wait()

    def turn(j, _):
        col = pl.multiple_of(j * 128, 128)
        for k in range(TOK // 128):
            part = cot[k * 128 : (k + 1) * 128, pl.ds(col, 128)].T
            sigt[pl.ds(col, 128), k * 128 : (k + 1) * 128] = (
                part.astype(F32) * tw[k : k + 1, :]
            ).astype(BF16)
        return 0

    lax.fori_loop(0, BLK // 128, turn, 0)
    loads[1].wait()
    for copy in loads[2:]:
        copy.start()

    def gradient_chunk(c):
        def rows(q, _):
            part = jnp.dot(
                sigt[pl.ds(pl.multiple_of(q * 320, 320), 320), :],
                inp[:, c * 256 : (c + 1) * 256],
                preferred_element_type=F32,
            )
            grad[q, :, :, c * 256 : (c + 1) * 256] = part.astype(BF16).reshape(4, SH, 256)
            return 0

        lax.fori_loop(0, 4, rows, 0)

    wview = wblk.reshape(4, 4, SH, BLK)
    sent = []

    def go(copy):
        copy.start()
        sent.append(copy)
        return copy

    F, B = 0, 2
    ylast, zlast, azlast, aylast = {}, {}, {}, {}

    def columns(c):
        return pl.ds(c * CW, CW)

    def own_part(c, block, side):
        return grad[side : side + 2, block, :, c * CW : (c + 1) * CW].astype(F32)

    def y_send(c, k, src, d):
        ylast[c, k] = go(send(src, ry.at[c, k], ysend.at[c, k], yrecv.at[c, k], at_y(d)))

    def reduce_a(c):
        if c % 2 == 0 and c > 0:
            gradient_chunk(c // 2)
        for k, block, side, d in ((0, 2, F, 1), (2, 2, B, 3), (1, 1, B, 1), (3, 3, F, 3)):
            y_send(c, k, grad.at[pl.ds(side, 2), (y + block) % 4, :, columns(c)], d)

    def reduce_b(c):
        for k, block, side, d in ((0, 1, F, 1), (2, 3, B, 3)):
            ylast[c, k].wait_recv()
            ry[c, k] = (ry[c, k].astype(F32) + own_part(c, (y + block) % 4, side)).astype(BF16)
            y_send(c, 4 + k // 2, ry.at[c, k], d)

    def reduce_z(c):
        for k, last, side in ((3, 4, F), (1, 5, B)):
            ylast[c, k].wait_recv()
            ylast[c, last].wait_recv()
            zacc[c, side : side + 2] = (
                own_part(c, y, side) + ry[c, k].astype(F32) + ry[c, last].astype(F32)
            ).astype(BF16)
        for d in (1, 2, 3):
            zlast[c, d] = go(
                send(
                    zacc.at[c, (z + d) % 4], rz.at[c, d - 1],
                    zsend.at[c, d - 1], zrecv.at[c, d - 1], at_z(d),
                )
            )

    started = []

    def adam(c):
        cols = slice(c * CW, (c + 1) * CW)
        total = zacc[c, z].astype(F32)
        for d in (1, 2, 3):
            zlast[c, d].wait_recv()
            total = total + rz[c, d - 1].astype(F32)
        if not started:
            for copy in loads[2:5]:
                copy.wait()
        started.append(c)
        gsum[:, cols] = total
        fresh = adam_update(total, wm[:, cols], m1[:, cols], m2[:, cols])[0]
        wblk[pl.ds(pl.multiple_of(fs * SH, 16), SH), cols] = fresh.astype(BF16)
        if len(started) == CHUNKS:
            store.start()
        place = wview.at[z, y, :, columns(c)]
        for d in (1, 2, 3):
            azlast[c, d] = go(send(place, place, azs.at[c, d - 1], azr.at[c, d - 1], at_z(d)))

    def gather_a(c):
        for d in (1, 2, 3):
            azlast[c, d].wait_recv()
        for k, d in ((0, 1), (1, 3)):
            place = wview.at[:, y, :, columns(c)]
            aylast[c, k] = go(send(place, place, ays.at[c, k], ayr.at[c, k], at_y(d)))

    def gather_b(c):
        for k, block, side, d in ((0, 3, F, 1), (1, 1, B, 3)):
            aylast[c, k].wait_recv()
            place = wview.at[pl.ds(side, 2), (y + block) % 4, :, columns(c)]
            aylast[c, k + 2] = go(
                send(place, place, ays.at[c, k + 2], ayr.at[c, k + 2], at_y(d))
            )

    def gather_end(c):
        aylast[c, 2].wait_recv()
        aylast[c, 3].wait_recv()

    stages = (reduce_a, reduce_b, reduce_z, adam, gather_a, gather_b, gather_end)
    store = pltpu.make_async_copy(gsum, gout_h, lsem.at[9])
    hcopies = [
        send(hsrc.at[(g + d) % 4], hbuf.at[g], hs_s.at[d - 1], hs_r.at[d - 1], at_g(d))
        for d in (1, 2, 3)
    ]
    def halves():
        h = hid[...]
        high = h.astype(BF16).astype(F32)
        return h, jnp.concatenate([high, h - high], axis=0).astype(BF16)

    def project(both, n, left, right):
        return lax.dot_general(
            both[:, left:right], wblk[n * 256 : (n + 1) * 256, left:right], NT,
            preferred_element_type=F32,
        )

    def put(s, part, left, right):
        part = part[0:8] + part[8:16]
        for i in range(4):
            qsend[s, i, :, left:right] = part[2 * i : 2 * i + 2]

    def gates_of(s, h, both):
        put(s, jnp.dot(both, sw[...], preferred_element_type=F32), BLK, BLK + 2 * NST)
        square = jnp.broadcast_to(jnp.sum(h * h, axis=1, keepdims=True), (8, 128))
        for i in range(4):
            qsend[s, i, :, BLK + 2 * NST :] = square[2 * i : 2 * i + 2]

    def query_of(s):
        h, both = halves()
        for n in range(BLK // 256):
            put(s, project(both, n, 0, BLK), n * 256, (n + 1) * 256)
        gates_of(s, h, both)

    def first_query():
        for copy in hcopies:
            copy.wait()
        for i in range(4):
            hid[2 * i : 2 * i + 2, :] = hbuf[i]
        for copy in loads[5:]:
            copy.wait()

        h, both = halves()
        gates_of(0, h, both)
        for n in range(BLK // 256):
            qacc[:, n * 256 : (n + 1) * 256] = project(both, n, 0, EARLY)

    gradient_chunk(0)
    pl.semaphore_wait(barrier, len(greeted))
    for t in range(LAG[-1] + CHUNKS):
        for stage, lag in list(zip(stages, LAG))[1:] + [(reduce_a, 0)]:
            if 0 <= t - lag < CHUNKS:
                stage(t - lag)
        if t == LAG[-1] + CHUNKS - 3:
            first_query()
        if t == 0:
            for copy in hcopies:
                copy.start()
            hbuf[g] = hsrc[g]

    _, both = halves()
    for n in range(BLK // 256):
        cols = slice(n * 256, (n + 1) * 256)
        put(0, qacc[:, cols] + project(both, n, EARLY, BLK), n * 256, (n + 1) * 256)

    head_of = (
        lax.broadcasted_iota(jnp.int32, (16, BLK), 1) // HEAD
        == lax.broadcasted_iota(jnp.int32, (16, BLK), 0)
    )
    own_row = lax.broadcasted_iota(jnp.int32, (16, BLK), 0)
    place128 = lax.broadcasted_iota(jnp.int32, (16, LC), 1)
    place16 = lax.broadcasted_iota(jnp.int32, (16, 16), 1)
    score_scale = 1.0 / math.sqrt(HEAD)

    def tp_copies(s):
        return [
            send(
                cbuf.at[s, tp], cbuf.at[s, tp], cs_s.at[s, d - 1], cs_r.at[s, d - 1], at_tp(d)
            )
            for d in (2, 1, 3)
        ]

    def decode_step(s, _, last=False):
        copies = [
            send(
                qsend.at[s, (g + d) % 4], qrecv.at[s, d - 1],
                qs_s.at[s, d - 1], qs_r.at[s, d - 1], at_g(d),
            )
            for d in (1, 2, 3)
        ]
        for copy in copies:
            copy.start()
        total = qsend[s, g]
        for d, copy in enumerate(copies):
            copy.wait_recv()
            total = total + qrecv[s, d]
        scale = lax.rsqrt(total[:, BLK + 2 * NST : BLK + 2 * NST + 1] * (1.0 / D) + norm_eps)
        query = total[:, 0:BLK] * scale
        gates = total[:, BLK : BLK + 2 * NST] * scale
        query_bf = query.astype(BF16).astype(F32)
        step_size = jnp.maximum(query, 0.0) + jnp.log1p(jnp.exp(-jnp.abs(query)))
        decay = jnp.exp(-dec[...] * step_size)
        drive = step_size * query

        in_gates = []
        for r in range(2):
            qrow = jnp.broadcast_to(query_bf[r : r + 1, :], (16, BLK))
            own_now = jnp.where(own_row == s, qrow, own[r])
            own[r] = own_now
            own_bf = own_now.astype(BF16)
            qhead = jnp.where(head_of, qrow, 0.0).astype(BF16)
            live = place128 < len_ref[r]
            mine_live = place16 <= s
            score = lax.dot_general(qhead, ck[r], NT, preferred_element_type=F32) * score_scale
            score_own = lax.dot_general(qhead, own_bf, NT, preferred_element_type=F32) * score_scale
            score = jnp.where(live, score, mask_fill)
            score_own = jnp.where(mine_live, score_own, mask_fill)
            top = jnp.maximum(
                jnp.max(score, axis=1, keepdims=True), jnp.max(score_own, axis=1, keepdims=True)
            )
            weight = jnp.where(live, jnp.exp(score - top), 0.0)
            weight_own = jnp.where(mine_live, jnp.exp(score_own - top), 0.0)
            norm = jnp.sum(weight, axis=1, keepdims=True) + jnp.sum(
                weight_own, axis=1, keepdims=True
            )
            prob = (weight / norm).astype(BF16)
            prob_own = (weight_own / norm).astype(BF16)
            attended = jnp.dot(prob, cv[r], preferred_element_type=F32) + jnp.dot(
                prob_own, own_bf, preferred_element_type=F32
            )
            attended = jnp.sum(jnp.where(head_of, attended, 0.0), axis=0, keepdims=True)
            in_row, out_row = gates[r : r + 1, 0:NST], gates[r : r + 1, NST:]
            out_gate = jnp.broadcast_to(out_row, (NST, NST)).T
            in_gates.append(in_row)
            both_gates = jnp.sum(in_row * out_row, axis=1, keepdims=True)
            for j in range(HEADS):
                cols = slice(j * 128, (j + 1) * 128)
                seen = jnp.sum(out_gate * st[r, :, cols], axis=0, keepdims=True)
                mixed = (
                    attended[:, cols]
                    + decay[r : r + 1, cols] * seen
                    + both_gates * drive[r : r + 1, cols]
                )
                mixbuf[s, g, r : r + 1, cols] = mixed.astype(BF16).astype(F32)

        copies2 = [
            send(
                mixbuf.at[s, g], mixbuf.at[s, g],
                ms_s.at[s, d - 1], ms_r.at[s, d - 1], at_g(d),
            )
            for d in (1, 2, 3)
        ]
        for copy in copies2:
            copy.start()
        for copy in copies:
            copy.wait_send()
        for r in range(0 if last else 2):
            in_gate = jnp.broadcast_to(in_gates[r], (NST, NST)).T
            for j in range(HEADS):
                cols = slice(j * 128, (j + 1) * 128)
                st[r, :, cols] = (
                    decay[r : r + 1, cols] * st[r, :, cols] + in_gate * drive[r : r + 1, cols]
                )
        for copy in copies2:
            copy.wait_recv()
        for i in range(4):
            mix8[2 * i : 2 * i + 2, :] = mixbuf[s, i]
        lhs = mix8[...].astype(BF16)
        part = [
            jnp.dot(lhs, wblk[:, half * 640 : (half + 1) * 640], preferred_element_type=F32)
            for half in range(2)
        ]
        if last:
            return part, copies2
        cbuf[s, tp] = jnp.concatenate(part, axis=0).astype(BF16)
        copies3 = tp_copies(s)
        for copy in copies3:
            copy.start()
        for copy in copies2:
            copy.wait_send()
        for copy in copies3:
            copy.wait_recv()
        total = (cbuf[s, 0].astype(F32) + cbuf[s, 1].astype(F32)) + (
            cbuf[s, 2].astype(F32) + cbuf[s, 3].astype(F32)
        )
        hid[:, 0:640] = hid[:, 0:640] + total[0:8]
        hid[:, 640:] = hid[:, 640:] + total[8:16]
        query_of(s + 1)
        return 0

    lax.fori_loop(0, STEPS - 1, decode_step, 0)
    part, pending = decode_step(STEPS - 1, 0, last=True)
    for half in range(2):
        cols = slice(half * 640, (half + 1) * 640)
        value = part[half] + jnp.where(tp == 0, hid[:, cols], 0.0)
        for i in range(4):
            fsrc[i, :, cols] = value[2 * i : 2 * i + 2]
    final = [
        send(
            fsrc.at[(g + dg) % 4], fbuf.at[g, tp],
            fs_s.at[dg, dt], fs_r.at[dg, dt], at_both(dg, dt),
        )
        for dg in (2, 1, 3, 0) for dt in (2, 3, 1, 0) if dg + dt > 0
    ]
    for copy in final:
        copy.start()
    fbuf[g, tp] = fsrc[g]
    store.wait()
    for copy in sent + pending:
        copy.wait_send()
    for s in range(STEPS - 1):
        for copy in tp_copies(s):
            copy.wait_send()
    for copy in final:
        copy.wait()
    for i in range(4):
        out_ref[:, i * BLK : (i + 1) * BLK] = (
            (fbuf[i, 0] + fbuf[i, 1]) + (fbuf[i, 2] + fbuf[i, 3])
        ).astype(BF16)


def on_device(
    learner_input, cotangent, token_ids, rewards, group_ids, weight_master, adam_first,
    adam_second, hidden_rows, cache_keys, cache_values, cache_lengths, ssm_state,
    state_weight, decay_rate,
):
    hbm = pl.BlockSpec(memory_space=pl.ANY)
    vmem = pl.BlockSpec(memory_space=pltpu.VMEM)
    smem = pl.BlockSpec(memory_space=pltpu.SMEM)
    dma = pltpu.SemaphoreType.DMA
    V = pltpu.VMEM
    shard = jax.ShapeDtypeStruct((SH, BLK), F32)
    rows = jax.ShapeDtypeStruct((2, D), BF16)
    grad, decoded = pl.pallas_call(
        kernel,
        out_shape=(shard, rows),
        in_specs=[hbm, hbm] + [vmem] * 3 + [hbm] * 3 + [vmem] + [hbm] * 2 + [smem] + [hbm] * 2 + [vmem],
        out_specs=(hbm, vmem),
        scratch_shapes=[
            V((TOK, BLK), BF16), V((TOK, BLK), BF16), V((BLK, TOK), BF16),
            V((4, 4, SH, BLK), BF16), V((BLK, BLK), BF16),
            V((CHUNKS, 6, 2, SH, CW), BF16), V((CHUNKS, 3, SH, CW), BF16),
            V((CHUNKS, 4, SH, CW), BF16),
            V((SH, BLK), F32), V((SH, BLK), F32), V((SH, BLK), F32), V((SH, BLK), F32),
            V((4, 2, BLK), F32), V((4, 2, BLK), F32),
            V((2, LC, BLK), BF16), V((2, LC, BLK), BF16), V((2, NST, BLK), F32),
            V((BLK, 2 * NST), BF16), V((1, BLK), F32),
            V((8, BLK), F32), V((16, BLK), F32), V((2, 16, BLK), F32),
            V((STEPS, 4, 2, QW), F32), V((STEPS, 3, 2, QW), F32),
            V((STEPS, 4, 2, BLK), F32), V((8, BLK), F32),
            V((STEPS, 4, 16, 640), BF16), V((4, 2, BLK), F32), V((4, 4, 2, BLK), F32),
            dma((10,)),
            dma((CHUNKS, 6)), dma((CHUNKS, 6)), dma((CHUNKS, 3)), dma((CHUNKS, 3)),
            dma((CHUNKS, 3)), dma((CHUNKS, 3)), dma((CHUNKS, 4)), dma((CHUNKS, 4)),
            dma((3,)), dma((3,)), dma((STEPS, 3)), dma((STEPS, 3)),
            dma((STEPS, 3)), dma((STEPS, 3)), dma((STEPS, 3)), dma((STEPS, 3)),
            dma((4, 4)), dma((4, 4)),
        ],
        compiler_params=pltpu.CompilerParams(
            collective_id=0, has_side_effects=True, vmem_limit_bytes=56 * 1024 * 1024
        ),
    )(
        learner_input, cotangent, token_ids.reshape(8, 128), rewards.reshape(1, 64),
        group_ids.reshape(1, 64), weight_master, adam_first, adam_second, hidden_rows,
        cache_keys, cache_values, cache_lengths, ssm_state, state_weight,
        decay_rate.reshape(HEADS, 128),
    )
    part = pl.BlockSpec((SH, BLK), lambda i: (0, i))
    whole = pl.BlockSpec((2, D), lambda i: (0, 0))
    return pl.pallas_call(
        finish,
        grid=(1,),
        out_shape=(shard, shard, shard, rows),
        in_specs=[part] * 4 + [whole],
        out_specs=(part, part, part, whole),
    )(grad, weight_master, adam_first, adam_second, decoded)


def solution(mesh):
    in_specs = (
        P("fsdp", "grp"), P("fsdp", "tp"), P("fsdp"), P(), P(),
        P(("tp", "fsdp"), "grp"), P(("tp", "fsdp"), "grp"), P(("tp", "fsdp"), "grp"),
        P(("fsdp", "grp"), None), P(("fsdp", "grp"), None, "tp"),
        P(("fsdp", "grp"), None, "tp"), P(("fsdp", "grp")),
        P(("fsdp", "grp"), None, "tp"), P(), P("tp"),
    )
    out_specs = (
        P(("tp", "fsdp"), "grp"), P(("tp", "fsdp"), "grp"), P(("tp", "fsdp"), "grp"),
        P(("fsdp", "grp"), None),
    )
    return jax.shard_map(
        on_device, mesh=mesh, in_specs=in_specs, out_specs=out_specs, check_vma=False
    )
```
